32 devices in a mesh: clus: 8 (over y, x, core), rep: 4 (over z).
Axes of the slice: x: 2, y: 2, z: 4, core: 2. Of those that a mesh axis runs over, the one named last changes fastest.
Arguments:
- nodes: bfloat16 [65536, 2048], P(('clus', 'rep')), may hold values from -6 to 6
- weight: bfloat16 [2048, 2048], P(('clus', 'rep')), may hold values from -0.125 to 0.125
- bias: bfloat16 [2048], P(('clus', 'rep')), may hold values from -3 to 3
- neighbours: int32 [65536, 16], P(('clus', 'rep')), may hold values from 0 to 2047, as said below
- degree: int32 [65536], P(('clus', 'rep')), may hold values from 0 to 16
- counts: int32 [32], P(('clus', 'rep')), may hold values from 614 to 2048, as said below
- cotangent: bfloat16 [65536, 2048], P(('clus', 'rep')), may hold values from -6 to 6
Outputs:
- activations: bfloat16 [65536, 2048], P(('clus', 'rep'))
- nodes_grad: bfloat16 [65536, 2048], P(('clus', 'rep'))
- weight_grad: float32 [2048, 2048], P(('clus', 'rep'))
- bias_grad: float32 [2048], P(('clus', 'rep'))
The draws below stay inside these ranges and needn't reach their ends.
Inputs may be any that keep to these rules, and one draw needn't show every extreme that they name: `counts`: one device's batch is full in every draw. `neighbours`: each entry is below its device's count.
All inputs are finite; a program needn't handle non-finite values.
Results may differ from the reference program's by a relative error of at most 0.0059.
Values may be sent and summed in bfloat16 or wider, within the bound.
No kernel may reach another device: no remote copies, remote signals or barrier semaphores. Data moves between devices by JAX's collectives and lax.ppermute only.
A program may use at most 192 MiB of HBM per device.

```python
import jax
import jax.numpy as jnp
from jax import lax

D = 2048
NODES_DEV = 2048
FAN = 16
NODES = 65536


def live_counts(key):
    devs = NODES // NODES_DEV
    first, second = jax.random.split(key)
    drawn = jax.random.randint(first, (devs,), NODES_DEV * 3 // 10, NODES_DEV + 1)
    full_one = jax.random.randint(second, (), 0, devs)
    return jnp.where(jnp.arange(devs) == full_one, NODES_DEV, drawn).astype(jnp.int32)


def draw_counts(key, part):
    return live_counts(key)


def draw_neighbours(key, part):
    limits = jnp.repeat(live_counts(key), NODES_DEV)[:, None]
    key = jax.random.fold_in(key, 7)
    return jax.random.randint(key, (NODES, FAN), 0, limits).astype(jnp.int32)


def touch_ends(entries, key, least, high):
    longest = entries.shape.index(max(entries.shape))
    spots = []
    for shift in (0, 1):
        where = [jax.random.randint(jax.random.fold_in(key, axis), (), 0, length) for axis, length in enumerate(entries.shape)]
        where[longest] = (where[longest] + shift) % entries.shape[longest]
        spots.append(tuple(where))
    return entries.at[spots[0]].set(least).at[spots[1]].set(high)


def with_spikes(result, key, source, target, blocks, factor):
    owner, partner = [(jnp.arange(result.shape[position]) // (result.shape[position] // blocks)).reshape([-1 if axis == position else 1 for axis in range(result.ndim)]) for position in (source, target)]
    chosen = jax.random.permutation(key, blocks)[partner]
    strong = (owner == chosen) | (owner == (partner + blocks // 2) % blocks)
    return jnp.where(strong, factor * result, result)


def levels(stream_key, extent, pieces, smallest, top_value):
    level, own = 1.0, jax.random.fold_in(stream_key, 6)
    for position, blocks in pieces:
        heights = jnp.exp(jax.random.uniform(jax.random.fold_in(own, position), (blocks,), jnp.float32, smallest / len(pieces), top_value / len(pieces)))
        level = level * jnp.repeat(heights, extent[position] // blocks).reshape([-1 if axis == position else 1 for axis in range(len(extent))])
    return level


def scatter_about(stream_key, extent, scale, limit, cuts=(), held_as=jnp.bfloat16):
    entries = scale * jax.random.normal(stream_key, extent, jnp.float32)
    if cuts:
        entries = entries * levels(stream_key, extent, cuts, -0.22, 0.18)
    return jnp.clip(entries, -limit, limit).astype(held_as)


def noise_with(own_key, extent, deviation, reach, cuts, heavy, kind=jnp.bfloat16):
    result = deviation * jax.random.normal(own_key, extent, jnp.float32)
    if cuts:
        result = result * levels(own_key, extent, cuts, -0.22, 0.18)
    return jnp.clip(with_spikes(result, jax.random.fold_in(own_key, 3), *heavy), -reach, reach).astype(kind)


def setup_inputs(seed: int = 0) -> dict:
    keys = jax.random.split(jax.random.key(seed), 8)
    nodes = noise_with(keys[0], (NODES, D), 1.0, 6.0, ((0, 32),), (0, 1, 32, 2.75))
    weight = scatter_about(keys[1], (D, D), D ** -0.5, 0.125, ((0, 32),))
    bias = scatter_about(keys[2], (D,), 0.5, 3.0, ((0, 32),))
    neighbours = draw_neighbours(jax.random.fold_in(keys[7], 71), 0)
    degree = touch_ends(jax.random.randint(keys[4], (NODES,), 0, FAN + 1), jax.random.fold_in(keys[4], 1), 0, FAN).astype(jnp.int32)
    counts = draw_counts(jax.random.fold_in(keys[7], 71), 0)
    cotangent = scatter_about(keys[6], (NODES, D), 1.0, 6.0, ((0, 32),))
    return {"nodes": nodes, "weight": weight, "bias": bias, "neighbours": neighbours, "degree": degree, "counts": counts, "cotangent": cotangent}


@jax.custom_vjp
def low(v):
    return lax.optimization_barrier(v.astype(jnp.bfloat16)).astype(jnp.float32)

@jax.custom_vjp
def low_back(v):
    return v

def low_keep(v):
    return (low(v), None)

def low_pass(kept, grad):
    return (grad,)

def back_keep(v):
    return (v, None)

def back_low(kept, grad):
    return (low(grad),)
low.defvjp(low_keep, low_pass)
low_back.defvjp(back_keep, back_low)

def aggregate_device(items):
    feats, lists, degs, count = items
    slots = jnp.arange(NODES_DEV, dtype=jnp.int32)
    live = (slots < count).astype(jnp.float32)
    scale = live / (degs.astype(jnp.float32) + 1.0)
    total = 2.0 * feats
    for k in range(FAN):
        valid = (k < degs)[:, None]
        total = total + jnp.where(valid, feats[lists[:, k]], 0.0)
    return total * scale[:, None]

def reference(nodes, weight, bias, neighbours, degree, counts, cotangent):
    devs = NODES // NODES_DEV
    lists = neighbours.reshape(devs, NODES_DEV, FAN)
    degs = degree.reshape(devs, NODES_DEV)
    slots = jnp.arange(NODES_DEV, dtype=jnp.int32)[None, :]
    live = (slots < counts[:, None]).astype(jnp.float32).reshape(NODES, 1)

    def forward(feats, wmat, bvec):
        agg = lax.map(jax.checkpoint(aggregate_device), (feats.reshape(devs, NODES_DEV, D), lists, degs, counts))
        agg = low_back(low(agg.reshape(NODES, D)))
        pre = jnp.dot(agg, wmat, precision=lax.Precision.HIGHEST, preferred_element_type=jnp.float32) + bvec
        pre = low_back(pre)
        return live * jax.nn.silu(pre)
    out, pullback = jax.vjp(forward, nodes.astype(jnp.float32), weight.astype(jnp.float32), bias.astype(jnp.float32))
    gx, gw, gb = pullback(cotangent.astype(jnp.float32))
    return (out.astype(jnp.bfloat16), gx.astype(jnp.bfloat16), gw, gb)
```

```python
import functools

import jax
import jax.numpy as jnp
from jax import lax
from jax.experimental import pallas as pl
from jax.experimental.pallas import tpu as pltpu
from jax.sharding import PartitionSpec as P

AXES = ("clus", "rep")
MIB = 2**20
F32 = jnp.float32
BF16 = jnp.bfloat16
Z1, Z2, CORE, X, Y = 1, 2, 4, 8, 16
ANY = pl.BlockSpec(memory_space=pl.ANY)
SMEM = pl.BlockSpec(memory_space=pltpu.SMEM)


def params(mib=48):
    return pltpu.CompilerParams(vmem_limit_bytes=mib * MIB)


def cost(flops, nbytes):
    return pl.CostEstimate(flops=flops, bytes_accessed=nbytes, transcendentals=0)


def column(row):
    return jnp.transpose(jnp.broadcast_to(row, (8, row.shape[1])))[:, :1]


def scale_row(start, degree, count):
    slots = start + lax.broadcasted_iota(jnp.int32, degree.shape, 1)
    live = (slots < count).astype(F32)
    return live / (degree.astype(F32) + 1.0)


def table_agg_kernel(count, nb, deg, nodes, table, agg):
    step = pl.program_id(0)
    n = nodes.shape[0]
    fan, tile = nb.shape
    degree = deg[...]
    start = step * tile
    chunk = 256
    used = lax.broadcasted_iota(jnp.int32, (fan, tile), 0) < degree
    slots = jnp.where(used, nb[...], -1)
    targets = lax.broadcasted_iota(jnp.int32, (chunk, tile), 0).astype(F32).astype(BF16)
    own = start + lax.broadcasted_iota(jnp.int32, (1, tile), 1)

    def local(rows, base):
        off = rows - base
        off = jnp.where(jnp.logical_and(off >= 0, off < chunk), off, -1)
        return off.astype(F32).astype(BF16)

    def build(c, carry):
        base = c * chunk
        here = local(slots, base)
        mine = local(own, base)
        one = jnp.ones((), BF16)
        zero = jnp.zeros((), BF16)
        acc = jnp.where(targets == mine, one + one, zero)
        for k in range(fan):
            acc = acc + jnp.where(targets == here[k : k + 1, :], one, zero)
        table[pl.ds(pl.multiple_of(base, chunk), chunk), :] = acc
        return carry

    lax.fori_loop(0, n // chunk, build, 0)
    total = lax.dot_general(table[...], nodes[...], (((0,), (0,)), ((), ())), preferred_element_type=F32)
    agg[...] = (total * column(scale_row(start, degree, count[0]))).astype(BF16)


def table_agg(count, nb, deg, nodes):
    n, d = nodes.shape
    fan = nb.shape[0]
    tile = 256
    return pl.pallas_call(
        table_agg_kernel,
        grid=(n // tile,),
        in_specs=[
            SMEM,
            pl.BlockSpec((fan, tile), lambda t: (0, t)),
            pl.BlockSpec((1, tile), lambda t: (0, t)),
            pl.BlockSpec((n, d), lambda t: (0, 0)),
        ],
        out_specs=[pl.BlockSpec((n, tile), lambda t: (0, t)), pl.BlockSpec((tile, d), lambda t: (t, 0))],
        out_shape=[jax.ShapeDtypeStruct((n, n), BF16), jax.ShapeDtypeStruct((n, d), BF16)],
        compiler_params=params(),
        cost_estimate=cost(3 * n * n * d, 3 * n * n * 2),
        name="table_agg",
    )(count, nb, deg, nodes)


def forward_kernel(count, agg, weight, bias, cot, act, grad, bias_sum):
    step = pl.program_id(0)
    tile = agg.shape[0]
    pre = jnp.dot(agg[...], weight[...], preferred_element_type=F32) + bias[...]
    slots = step * tile + lax.broadcasted_iota(jnp.int32, (tile, 1), 0)
    live = (slots < count[0]).astype(F32)
    sig = jax.nn.sigmoid(pre)
    act[...] = (live * pre * sig).astype(BF16)
    out = (cot[...].astype(F32) * live * sig * (1.0 + pre * (1.0 - sig))).astype(BF16)
    grad[...] = out
    part = jnp.sum(out.astype(F32), axis=0, keepdims=True)

    @pl.when(step == 0)
    def _():
        bias_sum[...] = part

    @pl.when(step > 0)
    def _():
        bias_sum[...] += part


def forward(count, agg, weight, bias, cot):
    n, d = agg.shape
    m = weight.shape[1]
    tile = 256
    row = pl.BlockSpec((tile, m), lambda t: (t, 0))
    return pl.pallas_call(
        forward_kernel,
        grid=(n // tile,),
        in_specs=[
            SMEM,
            pl.BlockSpec((tile, d), lambda t: (t, 0)),
            pl.BlockSpec((d, m), lambda t: (0, 0)),
            pl.BlockSpec((1, m), lambda t: (0, 0)),
            row,
        ],
        out_specs=[row, row, pl.BlockSpec((1, m), lambda t: (0, 0))],
        out_shape=[
            jax.ShapeDtypeStruct((n, m), BF16),
            jax.ShapeDtypeStruct((n, m), BF16),
            jax.ShapeDtypeStruct((1, m), F32),
        ],
        compiler_params=params(),
        cost_estimate=cost(2 * n * d * m, 5 * n * m * 2),
        name="forward",
    )(count, agg, weight, bias, cot)


def spread_rows(me, out, value):
    rows = value.shape[0] // 4
    z = lax.rem(me, 4)
    for q in range(4):
        place = pl.multiple_of(lax.bitwise_xor(z, q) * rows, rows)
        out[pl.ds(place, rows), :] = value[q * rows : (q + 1) * rows, :]


TN = (((0,), (0,)), ((), ()))


def wgrad_send_kernel(me, agg, grad, out):
    value = lax.dot_general(agg[...], grad[...], TN, preferred_element_type=F32)
    spread_rows(me[0], out.at[0], value.astype(BF16))


def wgrad_send(me, agg, grad):
    n, d = agg.shape
    m = grad.shape[1]
    tile = d // 8
    return pl.pallas_call(
        wgrad_send_kernel,
        grid_spec=pltpu.PrefetchScalarGridSpec(
            num_scalar_prefetch=1,
            grid=(4,),
            in_specs=[
                pl.BlockSpec((n, tile), lambda t, me: (0, (me[0] // 4) ^ (2 * t + 1))),
                pl.BlockSpec((n, m), lambda t, me: (0, 0)),
            ],
            out_specs=pl.BlockSpec((1, tile, m), lambda t, me: (t, 0, 0)),
        ),
        out_shape=jax.ShapeDtypeStruct((4, tile, m), BF16),
        compiler_params=params(),
        cost_estimate=cost(n * d * m, 2 * n * m * 2),
        name="wgrad_send",
    )(me, agg, grad)


def wgrad_keep_kernel(me, agg, grad, got, send_p, keep_p, send_q, keep_q, acc):
    t = pl.program_id(0)
    half = got.shape[2] // 2
    value = lax.dot_general(agg[...], grad[...], TN, preferred_element_type=F32)
    spread_rows(me[0], acc, value)
    for step in range(4):
        ry, rx = step // 2, step % 2

        @pl.when(t == step)
        def _():
            p = acc[:, :half] + got[0, :, :half].astype(F32)
            q = acc[:, half:] + got[0, :, half:].astype(F32)
            if ry:
                send_p[rx, :, :] = p.astype(BF16)
            else:
                keep_p[rx, :, :] = p
            if rx:
                send_q[ry, :, :] = q.astype(BF16)
            else:
                keep_q[ry, :, :] = q


def wgrad_keep(me, agg, grad, got):
    n, d = agg.shape
    m = grad.shape[1]
    tile = d // 8
    whole = pl.BlockSpec((2, tile, m // 2), lambda t, me: (0, 0, 0))
    low = jax.ShapeDtypeStruct((2, tile, m // 2), BF16)
    wide = jax.ShapeDtypeStruct((2, tile, m // 2), F32)
    return pl.pallas_call(
        wgrad_keep_kernel,
        grid_spec=pltpu.PrefetchScalarGridSpec(
            num_scalar_prefetch=1,
            grid=(4,),
            in_specs=[
                pl.BlockSpec((n, tile), lambda t, me: (0, (me[0] // 4) ^ (2 * t))),
                pl.BlockSpec((n, m), lambda t, me: (0, 0)),
                pl.BlockSpec((1, tile, m), lambda t, me: (t, 0, 0)),
            ],
            out_specs=[whole] * 4,
            scratch_shapes=[pltpu.VMEM((tile, m), F32)],
        ),
        out_shape=[low, wide, low, wide],
        compiler_params=params(),
        cost_estimate=cost(n * d * m, 3 * n * m * 2),
        name="wgrad_keep",
    )(me, agg, grad, got)


def agg_grad_kernel(first, count, deg, grad, weight, out):
    tile = grad.shape[0]
    value = lax.dot_general(grad[...], weight[...], (((1,), (1,)), ((), ())), preferred_element_type=F32)
    start = (pl.program_id(0) + first) * tile
    out[...] = (value * column(scale_row(start, deg[...], count[0]))).astype(BF16)


def agg_grad(count, deg, grad, weight, first, steps):
    m = grad.shape[1]
    d = weight.shape[0]
    tile = 256
    return pl.pallas_call(
        functools.partial(agg_grad_kernel, first),
        grid=(steps,),
        in_specs=[
            SMEM,
            pl.BlockSpec((1, tile), lambda t: (0, t + first)),
            pl.BlockSpec((tile, m), lambda t: (t + first, 0)),
            pl.BlockSpec((d, m), lambda t: (0, 0)),
        ],
        out_specs=pl.BlockSpec((tile, d), lambda t: (t, 0)),
        out_shape=jax.ShapeDtypeStruct((steps * tile, d), BF16),
        compiler_params=params(),
        cost_estimate=cost(2 * steps * tile * d * m, (d + 2 * steps * tile) * m * 2),
        name="agg_grad",
    )(count, deg, grad, weight)


def nodes_grad_kernel(table, low, high, *rest):
    out = rest[-1]
    half = low.shape[0]
    value = jnp.dot(table[:, :half], low[...], preferred_element_type=F32)
    value = value + jnp.dot(table[:, half:], high[...], preferred_element_type=F32)
    out[...] = value.astype(BF16)


def nodes_grad(table, low, high, first, steps, into=None):
    n = table.shape[0]
    d = low.shape[1]
    tile = 256
    whole = pl.BlockSpec(low.shape, lambda t: (0, 0))
    extra = [] if into is None else [into]
    return pl.pallas_call(
        nodes_grad_kernel,
        grid=(steps,),
        in_specs=[pl.BlockSpec((tile, n), lambda t: (t + first, 0)), whole, whole] + [ANY] * len(extra),
        out_specs=pl.BlockSpec((tile, d), lambda t: (t + first, 0)),
        out_shape=jax.ShapeDtypeStruct((n, d), BF16),
        input_output_aliases={3: 0} if extra else {},
        compiler_params=params(),
        cost_estimate=cost(2 * steps * tile * d * n, (n + 2 * steps * tile) * d * 2),
        name="nodes_grad",
    )(table, low, high, *extra)


def swap(value, bit):
    return lax.ppermute(value, AXES, [(i, i ^ bit) for i in range(32)])


def place_kernel(codes, me, *refs):
    pieces, out, sem = refs[:-2], refs[-2], refs[-1]
    copies = []
    for (order, col), piece in zip(codes, pieces):
        rows = piece.shape[0] // len(order)
        for i, code in enumerate(order):
            at = pl.multiple_of(lax.bitwise_xor(me[0], code) * rows, rows)
            copies.append(
                pltpu.make_async_copy(
                    piece.at[pl.ds(i * rows, rows), :],
                    out.at[pl.ds(at, rows), pl.ds(col, piece.shape[1])],
                    sem.at[len(copies)],
                )
            )
    for c in copies:
        c.start()
    for c in copies:
        c.wait()


def place(me, pieces, codes, shape):
    total = sum(len(order) for order, _ in codes)
    return pl.pallas_call(
        functools.partial(place_kernel, codes),
        in_specs=[SMEM] + [ANY] * len(pieces),
        out_specs=ANY,
        out_shape=jax.ShapeDtypeStruct(shape, pieces[0].dtype),
        scratch_shapes=[pltpu.SemaphoreType.DMA((total,))],
        compiler_params=params(8),
        cost_estimate=cost(0, 4 * shape[0] * shape[1]),
        name="place",
    )(me, *pieces)


def gather_z(block):
    one, two = swap(block, Z1), swap(block, Z2)
    return jnp.concatenate([block, one, two, swap(two, Z1)], axis=0)


def gather(block, bit):
    return jnp.concatenate([block, swap(block, bit)], axis=0)


def codes_of(*bits):
    order = [0]
    for group in bits:
        order = [code ^ g for g in group for code in order]
    return order


ZS = (0, Z1, Z2, Z1 ^ Z2)


def gather_weight(me, weight):
    half = weight.shape[1] // 2
    p = gather_z(gather(gather(weight[:, :half], X), Y))
    q = gather(gather(gather_z(weight[:, half:]), X), Y)
    order_p = codes_of((0, X), (0, Y), ZS)
    order_q = codes_of(ZS, (0, X), (0, Y))
    codes = (
        (order_p, 0),
        ([c ^ CORE for c in order_p], 0),
        (order_q, half),
        ([c ^ CORE for c in order_q], half),
    )
    rows = 32 * weight.shape[0]
    return place(me, (p, swap(p, CORE), q, swap(q, CORE)), codes, (rows, 2 * half))


def gather_bias(me, bias):
    block = bias[None, :]
    for bit in (CORE, X, Y, Z2, Z1):
        block = gather(block, bit)
    order = jnp.array(codes_of((0, CORE), (0, X), (0, Y), (0, Z2), (0, Z1)), jnp.int32)
    inverse = jnp.argsort(order) if False else order
    del inverse
    position = [0] * 32
    for i, code in enumerate(codes_of((0, CORE), (0, X), (0, Y), (0, Z2), (0, Z1))):
        position[code] = i
    wanted = jnp.bitwise_xor(jnp.arange(32, dtype=jnp.int32), me[0])
    return block[jnp.array(position, jnp.int32)[wanted]].reshape(1, -1)


def scatter_weight(send_p, keep_p, send_q, keep_q, rows):
    got_p, got_q = swap(send_p, Y), swap(send_q, X)
    next_p = (keep_p[1] + got_p[1].astype(F32)).astype(BF16)
    next_q = (keep_q[1] + got_q[1].astype(F32)).astype(BF16)
    got2_p, got2_q = swap(next_p, X), swap(next_q, Y)
    p = keep_p[0] + got_p[0].astype(F32) + got2_p.astype(F32)
    q = keep_q[0] + got_q[0].astype(F32) + got2_q.astype(F32)

    def piece(i):
        return jnp.concatenate([p[i * rows : (i + 1) * rows], q[i * rows : (i + 1) * rows]], axis=1)

    far = swap(piece(3).astype(BF16), Z1)
    near = swap(piece(1).astype(BF16), Z1)
    mid = swap((piece(2) + far.astype(F32)).astype(BF16), Z2)
    return piece(0) + near.astype(F32) + mid.astype(F32)


def sum_bias(me, part, rows):
    for bit in (CORE, X, Y, Z2, Z1):
        part = part + swap(part, bit)
    return lax.dynamic_slice_in_dim(part[0], me[0] * rows, rows, 0)


def fast(nodes, weight, bias, neighbours, degree, counts, cotangent):
    me = (lax.axis_index("clus") * 4 + lax.axis_index("rep")).astype(jnp.int32)[None]
    rows = weight.shape[0]
    nb = neighbours.T
    deg = degree[None, :]
    full = gather_weight(me, weight)
    bias_full = gather_bias(me, bias).astype(F32)
    table, agg = table_agg(counts, nb, deg, nodes)
    act, grad, bias_part = forward(counts, agg, full, bias_full, cotangent)
    terms = wgrad_send(me, agg, grad)
    got = swap(terms, CORE)
    steps = nodes.shape[0] // 512
    low = agg_grad(counts, deg, grad, full, 0, steps)
    parts = wgrad_keep(me, agg, grad, got)
    high = agg_grad(counts, deg, grad, full, steps, steps)
    weight_grad = scatter_weight(*parts, rows)
    bias_grad = sum_bias(me, bias_part, rows)
    first = nodes_grad(table, low, high, 0, steps)
    out = nodes_grad(table, low, high, steps, steps, first)
    return act, out, weight_grad, bias_grad


def general(nodes, weight, bias, neighbours, degree, counts, cotangent):
    nb = neighbours.T
    deg = degree[None, :]
    full = lax.all_gather(weight, AXES, axis=0, tiled=True)
    bias_full = lax.all_gather(bias, AXES, axis=0, tiled=True).astype(F32)[None, :]
    table, agg = table_agg(counts, nb, deg, nodes)
    act, grad, bias_part = forward(counts, agg, full, bias_full, cotangent)
    term = lax.dot_general(agg, grad, TN, preferred_element_type=F32)
    weight_grad = lax.psum_scatter(term, AXES, scatter_dimension=0, tiled=True)
    bias_grad = lax.psum_scatter(bias_part[0], AXES, scatter_dimension=0, tiled=True)
    steps = nodes.shape[0] // 512
    low = agg_grad(counts, deg, grad, full, 0, steps)
    high = agg_grad(counts, deg, grad, full, steps, steps)
    first = nodes_grad(table, low, high, 0, steps)
    out = nodes_grad(table, low, high, steps, steps, first)
    return act, out, weight_grad, bias_grad


def solution(mesh):
    both = P(AXES, None)
    one = P(AXES)
    cube = (mesh.shape["clus"], mesh.shape["rep"]) == (8, 4)
    return jax.shard_map(
        fast if cube else general,
        mesh=mesh,
        in_specs=(both, both, one, both, one, one, both),
        out_specs=(both, both, both, one),
        check_vma=False,
    )
```

```python
import functools

import jax
import jax.numpy as jnp
from jax import lax
from jax.experimental import pallas as pl
from jax.experimental.pallas import tpu as pltpu
from jax.sharding import PartitionSpec as P

AXES = ("clus", "rep")
MIB = 2**20
F32 = jnp.float32
BF16 = jnp.bfloat16
Z1, Z2, CORE, X, Y = 1, 2, 4, 8, 16
ANY = pl.BlockSpec(memory_space=pl.ANY)
SMEM = pl.BlockSpec(memory_space=pltpu.SMEM)
TN = (((0,), (0,)), ((), ()))
NT = (((1,), (1,)), ((), ()))
NN = (((1,), (0,)), ((), ()))
VMEM = pl.BlockSpec(memory_space=pltpu.VMEM)
HBM = pl.BlockSpec(memory_space=pltpu.HBM)
EXTRA = 128


def params(mib=12):
    return pltpu.CompilerParams(vmem_limit_bytes=int(mib * MIB))


def cost(flops, nbytes):
    return pl.CostEstimate(flops=flops, bytes_accessed=nbytes, transcendentals=0)


def column(row):
    return jnp.transpose(jnp.broadcast_to(row, (8, row.shape[1])))[:, :1]


def scale_row(start, degree, count):
    slots = start + lax.broadcasted_iota(jnp.int32, degree.shape, 1)
    live = (slots < count).astype(F32)
    return live / (degree.astype(F32) + 1.0)


def table_kernel(first, ctl, nb, deg, *rest):
    table, ctl_out = rest[-2:]
    hand_on(ctl, ctl_out)
    n = table.shape[0]
    fan, tile = nb.shape
    start = (pl.program_id(0) + first) * tile
    chunk = 256
    used = lax.broadcasted_iota(jnp.int32, (fan, tile), 0) < deg[...]
    slots = jnp.where(used, nb[...], -1)
    targets = lax.broadcasted_iota(jnp.int32, (chunk, tile), 0).astype(F32).astype(BF16)
    own = start + lax.broadcasted_iota(jnp.int32, (1, tile), 1)
    one = jnp.ones((), BF16)
    zero = jnp.zeros((), BF16)

    def local(rows, base):
        off = rows - base
        off = jnp.where(jnp.logical_and(off >= 0, off < chunk), off, -1)
        return off.astype(F32).astype(BF16)

    def build(c, carry):
        base = c * chunk
        here = local(slots, base)
        acc = jnp.where(targets == local(own, base), one + one, zero)
        for k in range(fan):
            acc = acc + jnp.where(targets == here[k : k + 1, :], one, zero)
        table[pl.ds(pl.multiple_of(base, chunk), chunk), :] = acc
        return carry

    lax.fori_loop(0, n // chunk, build, 0)


def neighbour_table(ctl, nb, deg, first, steps, into=None):
    fan, n = nb.shape
    tile = n // 4
    extra = [] if into is None else [into]
    return pl.pallas_call(
        functools.partial(table_kernel, first),
        grid=(steps,),
        in_specs=[
            SMEM,
            pl.BlockSpec((fan, tile), lambda t: (0, t + first)),
            pl.BlockSpec((1, tile), lambda t: (0, t + first)),
        ]
        + [ANY] * len(extra),
        out_specs=[pl.BlockSpec((n, tile), lambda t: (0, t + first)), SMEM],
        out_shape=[jax.ShapeDtypeStruct((n, n), BF16), CTL],
        input_output_aliases={3: 0} if extra else {},
        compiler_params=params(6),
        cost_estimate=cost(n * n * tile * steps, n * tile * steps * 2),
        name="table",
    )(ctl, nb, deg, *extra)


TILE = 256


def columns_of(ref, t):
    return ref[:, pl.ds(pl.multiple_of(t * TILE, TILE), TILE)]


def scaled(ctl, deg, t, value):
    at = pl.multiple_of(t * TILE, TILE)
    return (value * column(scale_row(at, deg[:, pl.ds(at, TILE)], ctl[1]))).astype(BF16)


CTL = jax.ShapeDtypeStruct((2,), jnp.int32)


def hand_on(ctl, ctl_out):
    ctl_out[0] = ctl[0]
    ctl_out[1] = ctl[1]


def rows_spec(width, first=0):
    return pl.BlockSpec((TILE, width), lambda t: (t + first, 0))


def aggregate_kernel(first, ctl, deg, table, nodes, *rest):
    out, ctl_out = rest[-2:]
    hand_on(ctl, ctl_out)
    t = pl.program_id(0) + first
    value = lax.dot_general(columns_of(table, t), nodes[...], TN, preferred_element_type=F32)
    out[...] = scaled(ctl, deg, t, value)


def aggregate(ctl, deg, table, nodes, first, steps, into=None):
    n, d = nodes.shape
    extra = [] if into is None else [into]
    return pl.pallas_call(
        functools.partial(aggregate_kernel, first),
        grid=(steps,),
        in_specs=[SMEM, VMEM, VMEM, VMEM] + [ANY] * len(extra),
        out_specs=[rows_spec(d, first), SMEM],
        out_shape=[jax.ShapeDtypeStruct((n, d), BF16), CTL],
        input_output_aliases={4: 0} if extra else {},
        compiler_params=params(3),
        cost_estimate=cost(2 * steps * TILE * d * n, (n + 2 * steps * TILE) * d * 2),
        name="aggregate",
    )(ctl, deg, table, nodes, *extra)


def forward_kernel(ctl, agg, weight, bias, cot_all, act, grad, bias_sum, ctl_out, cot_v, cot_sem):
    hand_on(ctl, ctl_out)
    t = pl.program_id(0)
    half = weight.shape[1] // 2

    def fetch(i):
        slot = lax.rem(i, 2)
        rows = pl.ds(pl.multiple_of(i * TILE, TILE), TILE)
        return pltpu.make_async_copy(cot_all.at[rows, :], cot_v.at[slot], cot_sem.at[slot])

    @pl.when(t == 0)
    def _():
        bias_sum[...] = jnp.zeros_like(bias_sum)
        fetch(t).start()

    fetch(t).wait()

    @pl.when(t + 1 < pl.num_programs(0))
    def _():
        fetch(t + 1).start()

    cot = cot_v.at[lax.rem(t, 2)]

    slots = t * TILE + lax.broadcasted_iota(jnp.int32, (TILE, half), 0)
    live = (slots < ctl[1]).astype(F32).astype(BF16)
    for side in range(2):
        at = slice(side * half, (side + 1) * half)
        pre = jnp.dot(agg[...], weight[:, at], preferred_element_type=F32) + bias[:, at]
        sig = jax.nn.sigmoid(pre)
        silu = pre * sig
        act[:, at] = silu.astype(BF16) * live
        slope = (cot[:, at] * live).astype(F32) * (sig + silu * (1.0 - sig))
        grad[:, at] = slope.astype(BF16)
        bias_sum[:, at] += jnp.sum(slope, axis=0, keepdims=True)


def forward(ctl, agg, weight, bias, cot):
    n, d = agg.shape
    m = weight.shape[1]
    return pl.pallas_call(
        forward_kernel,
        grid=(n // TILE,),
        in_specs=[SMEM, rows_spec(d), VMEM, VMEM, HBM],
        out_specs=[rows_spec(m), rows_spec(m), VMEM, SMEM],
        out_shape=[
            jax.ShapeDtypeStruct((n, m), BF16),
            jax.ShapeDtypeStruct((n, m), BF16),
            jax.ShapeDtypeStruct((1, m), F32),
            CTL,
        ],
        scratch_shapes=[pltpu.VMEM((2, TILE, m), BF16), pltpu.SemaphoreType.DMA((2,))],
        compiler_params=params(14),
        cost_estimate=cost(2 * n * d * m, 5 * n * m * 2),
        name="forward",
    )(ctl, agg, weight, bias, cot)


def place_kernel(codes, ctl, *refs):
    pieces, refs = refs[: len(codes)], refs[len(codes) :]
    weight, bias, ctl_out, heads, weight_sem, head_sem = refs[-6:]
    hand_on(ctl, ctl_out)
    m = weight.shape[1]
    copies, head_copies, pairs = [], [], []
    for (order, col), piece in zip(codes, pieces):
        rows = piece.shape[0] // len(order)
        wide = min(piece.shape[1], m - col)
        for i, code in enumerate(order):
            owner = lax.bitwise_xor(ctl[0], code)
            copies.append(
                pltpu.make_async_copy(
                    piece.at[pl.ds(i * rows, rows), pl.ds(0, wide)],
                    weight.at[pl.ds(pl.multiple_of(owner * rows, rows), rows), pl.ds(col, wide)],
                    weight_sem.at[len(copies)],
                )
            )
            if wide < piece.shape[1]:
                head = piece.at[pl.ds(i * rows, 16), pl.ds(wide, EXTRA)]
                k = len(head_copies)
                head_copies.append(pltpu.make_async_copy(head, heads.at[k], head_sem.at[k]))
                if code & 1 == 0:
                    pairs.append((k, order.index(code ^ 1) - i + k, owner // 2))
    for c in copies + head_copies:
        c.start()
    bias[...] = refs[1][...] if len(refs) == 8 else jnp.zeros_like(bias)
    for c in head_copies:
        c.wait()
    for one, two, pair in pairs:
        both = heads[one, :1, :].astype(F32) + heads[two, :1, :].astype(F32)
        bias[:, pl.ds(pl.multiple_of(pair * EXTRA, EXTRA), EXTRA)] = both
    for c in copies:
        c.wait()


def place(ctl, pieces, codes, shape, into=()):
    total = sum(len(order) for order, _ in codes)
    first = 1 + len(pieces)
    return pl.pallas_call(
        functools.partial(place_kernel, codes),
        in_specs=[SMEM] + [ANY] * len(pieces) + ([ANY, VMEM] if into else []),
        out_specs=[ANY, VMEM, SMEM],
        out_shape=[jax.ShapeDtypeStruct(shape, BF16), jax.ShapeDtypeStruct((1, shape[1]), F32), CTL],
        input_output_aliases={first: 0} if into else {},
        scratch_shapes=[
            pltpu.VMEM((total // 2, 16, EXTRA), BF16),
            pltpu.SemaphoreType.DMA((total,)),
            pltpu.SemaphoreType.DMA((total // 2,)),
        ],
        compiler_params=params(1),
        cost_estimate=cost(0, 2 * shape[0] * shape[1]),
        name="place",
    )(ctl, *pieces, *into)


def terms_of(me, tile, value, bias_sum, out):
    m = value.shape[1]
    rows = value.shape[0] // 4
    z = lax.rem(me, 4)
    out[:, m:] = jnp.zeros((value.shape[0], EXTRA), BF16)
    head = lax.broadcasted_iota(jnp.int32, (16, EXTRA), 0) == 0
    for q in range(4):
        at = pl.multiple_of(lax.bitwise_xor(z, q) * rows, rows)
        out[pl.ds(at, rows), :m] = value[q * rows : (q + 1) * rows, :].astype(BF16)
        pair = bias_sum[:, pl.ds(pl.multiple_of(tile * TILE + q // 2 * EXTRA, EXTRA), EXTRA)]
        out[pl.ds(at, 16), m:] = jnp.where(head, pair, 0.0).astype(BF16)


def wgrad_kernel(other, ctl, agg, grad, bias_sum, out, ctl_out):
    hand_on(ctl, ctl_out)
    tile = lax.bitwise_xor(ctl[0] // 4, 2 * pl.program_id(0) + other)
    value = lax.dot_general(columns_of(agg, tile), grad[...], TN, preferred_element_type=F32)
    terms_of(ctl[0], tile, value, bias_sum, out.at[0])


def wgrad(ctl, agg, grad, bias_sum, other):
    n, d = agg.shape
    m = grad.shape[1]
    return pl.pallas_call(
        functools.partial(wgrad_kernel, other),
        grid=(4,),
        in_specs=[SMEM, VMEM, VMEM, VMEM],
        out_specs=[pl.BlockSpec((1, TILE, m + EXTRA), lambda t: (t, 0, 0)), SMEM],
        out_shape=[jax.ShapeDtypeStruct((4, TILE, m + EXTRA), BF16), CTL],
        compiler_params=params(5),
        cost_estimate=cost(n * d * m, 2 * n * m * 2),
        name="wgrad",
    )(ctl, agg, grad, bias_sum)


def agg_grad_kernel(ctl, deg, grad, weight, out, ctl_out):
    hand_on(ctl, ctl_out)
    value = lax.dot_general(grad[...], weight[...], NT, preferred_element_type=F32)
    out[...] = scaled(ctl, deg, pl.program_id(0), value)


def agg_grad(ctl, deg, grad, weight):
    n, m = grad.shape
    d = weight.shape[0]
    return pl.pallas_call(
        agg_grad_kernel,
        grid=(n // TILE,),
        in_specs=[SMEM, VMEM, rows_spec(m), VMEM],
        out_specs=[rows_spec(d), SMEM],
        out_shape=[jax.ShapeDtypeStruct((n, d), BF16), CTL],
        compiler_params=params(3),
        cost_estimate=cost(2 * n * d * m, 3 * n * m * 2),
        name="agg_grad",
    )(ctl, deg, grad, weight)


def nodes_grad_kernel(ctl, table, spread, *rest):
    out, ctl_out = rest[-2:]
    hand_on(ctl, ctl_out)
    out[...] = jnp.dot(table[...], spread[...], preferred_element_type=F32).astype(BF16)


def nodes_grad(ctl, table, spread, first, steps, into=None):
    n, d = spread.shape
    extra = [] if into is None else [into]
    return pl.pallas_call(
        nodes_grad_kernel,
        grid=(steps,),
        in_specs=[SMEM, rows_spec(n, first), VMEM] + [ANY] * len(extra),
        out_specs=[rows_spec(d, first), SMEM],
        out_shape=[jax.ShapeDtypeStruct((n, d), BF16), CTL],
        input_output_aliases={3: 0} if extra else {},
        compiler_params=params(4),
        cost_estimate=cost(2 * steps * TILE * d * n, (n + 2 * steps * TILE) * d * 2),
        name="nodes_grad",
    )(ctl, table, spread, *extra)


def swap(value, bit):
    return lax.ppermute(value, AXES, [(i, i ^ bit) for i in range(32)])


def after(value, *others):
    return lax.optimization_barrier((value, *others))[0]


def codes_of(*bits):
    order = [0]
    for group in bits:
        order = [code ^ g for g in group for code in order]
    return order


def with_bias(odd, weight, bias):
    rows = bias.shape[0]
    lanes = jnp.concatenate([bias, bias])
    mine = (jnp.arange(EXTRA) >= rows) == odd
    head = jnp.where(mine, lanes, 0).astype(BF16)[None, :]
    tail = jnp.where(jnp.arange(rows)[:, None] == 0, head, 0).astype(BF16)
    return jnp.concatenate([weight, tail], axis=1)


def cat(*parts):
    return jnp.concatenate(parts, axis=0)


def fast(nodes, weight, bias, neighbours, degree, counts, cotangent):
    me = (lax.axis_index("clus") * 4 + lax.axis_index("rep")).astype(jnp.int32)[None]
    ctl = cat(me, counts)
    rows, m = weight.shape
    half = m // 2
    nb = neighbours.T
    deg = degree[None, :]
    steps = nodes.shape[0] // TILE

    odd = me % 2 == 1
    own = with_bias(odd, weight, bias)
    one, two = swap(own, Z1), swap(own, Z2)
    table, ctl = neighbour_table(after(ctl, own), nb, deg, 0, 3)
    one, two = after(one, ctl), after(two, ctl)
    three = swap(two, Z1)
    table, ctl = neighbour_table(after(ctl, two), nb, deg, 3, 1, table)
    three = after(three, ctl)
    p = cat(own[:, :half], one[:, :half], two[:, :half], three[:, :half])
    q = cat(own[:, half:], one[:, half:], two[:, half:], three[:, half:])
    px, qy = swap(p, X), swap(q, Y)
    agg, ctl = aggregate(after(ctl, p, q), deg, table, nodes, 0, 3)
    px, qy = after(px, ctl), after(qy, ctl)
    p, q = cat(p, px), cat(q, qy)
    py, qx = swap(p, Y), swap(q, X)
    p_other, q_other = swap(p, CORE), swap(q, CORE)
    agg, ctl = aggregate(after(ctl, p, q), deg, table, nodes, 3, steps - 3, agg)
    zs = (0, Z1, Z2, Z1 ^ Z2)
    near_p, near_q = codes_of(zs, (0, X)), codes_of(zs, (0, Y))

    def ends(flip_p, flip_q):
        order_p, order_q = [c ^ flip_p for c in near_p], [c ^ flip_q for c in near_q]
        return (order_p, 0), (order_q, half), ([c ^ CORE for c in order_p], 0), ([c ^ CORE for c in order_q], half)

    *full, ctl = place(ctl, (p, q, p_other, q_other), ends(0, 0), (32 * rows, m))
    py, qx = after(py, ctl), after(qx, ctl)
    pieces = (py, qx, swap(py, CORE), swap(qx, CORE))
    full, bias_full, ctl = place(ctl, pieces, ends(Y, X), (32 * rows, m), full)
    act, grad, bias_sum, ctl = forward(ctl, agg, full, bias_full, cotangent)

    terms, ctl = wgrad(ctl, agg, grad, bias_sum, 1)
    got = swap(terms, CORE)
    mine, ctl = wgrad(ctl, agg, grad, bias_sum, 0)
    got = after(got, ctl).reshape(2, 2, 4 * rows, m + EXTRA)
    mine = mine.reshape(2, 2, 4 * rows, m + EXTRA)

    def total(*parts):
        return functools.reduce(jnp.add, [part.astype(F32) for part in parts])

    send_p = total(mine[1, :, :, :half], got[1, :, :, :half]).astype(BF16)
    send_q = total(mine[:, 1, :, half:], got[:, 1, :, half:]).astype(BF16)
    got_p, got_q = swap(send_p, Y), swap(send_q, X)
    spread, ctl = agg_grad(after(ctl, send_p, send_q), deg, grad, full)
    got_p, got_q = after(got_p, ctl), after(got_q, ctl)
    next_p = total(mine[0, 1, :, :half], got[0, 1, :, :half], got_p[1]).astype(BF16)
    next_q = total(mine[1, 0, :, half:], got[1, 0, :, half:], got_q[1]).astype(BF16)
    got2_p, got2_q = swap(next_p, X), swap(next_q, Y)
    out, ctl = nodes_grad(after(ctl, next_p, next_q), table, spread, 0, 3)
    got2_p, got2_q = after(got2_p, ctl), after(got2_q, ctl)

    def piece(i):
        at = slice(i * rows, (i + 1) * rows)
        p = total(mine[0, 0, at, :half], got[0, 0, at, :half], got_p[0, at], got2_p[at])
        q = total(mine[0, 0, at, half:], got[0, 0, at, half:], got_q[0, at], got2_q[at])
        return jnp.concatenate([p, q], axis=1)

    third, first = piece(3).astype(BF16), piece(1).astype(BF16)
    far, near = swap(third, Z1), swap(first, Z1)
    out, ctl = nodes_grad(after(ctl, third, first), table, spread, 3, 2, out)
    second = (piece(2) + after(far, ctl).astype(F32)).astype(BF16)
    mid = swap(second, Z2)
    out, ctl = nodes_grad(after(ctl, second), table, spread, 5, steps - 5, out)
    near, mid = after(near, ctl), after(mid, ctl)
    last = piece(0) + near.astype(F32) + mid.astype(F32)
    bias_grad = jnp.where(odd, last[0, m + rows :], last[0, m : m + rows])
    return act, out, last[:, :m], bias_grad


def general(nodes, weight, bias, neighbours, degree, counts, cotangent):
    ctl = cat(jnp.zeros_like(counts), counts)
    nb = neighbours.T
    deg = degree[None, :]
    steps = nodes.shape[0] // TILE
    full = lax.all_gather(weight, AXES, axis=0, tiled=True)
    bias_full = lax.all_gather(bias, AXES, axis=0, tiled=True).astype(F32)[None, :]
    table, _ = neighbour_table(ctl, nb, deg, 0, 4)
    agg, _ = aggregate(ctl, deg, table, nodes, 0, steps)
    act, grad, bias_sum, _ = forward(ctl, agg, full, bias_full, cotangent)
    term = lax.dot_general(agg, grad, TN, preferred_element_type=F32)
    weight_grad = lax.psum_scatter(term, AXES, scatter_dimension=0, tiled=True)
    bias_grad = lax.psum_scatter(bias_sum[0], AXES, scatter_dimension=0, tiled=True)
    spread, _ = agg_grad(ctl, deg, grad, full)
    out, _ = nodes_grad(ctl, table, spread, 0, steps)
    return act, out, weight_grad, bias_grad


def solution(mesh):
    both = P(AXES, None)
    one = P(AXES)
    cube = (mesh.shape["clus"], mesh.shape["rep"]) == (8, 4)
    return jax.shard_map(
        fast if cube else general,
        mesh=mesh,
        in_specs=(both, both, one, both, one, one, both),
        out_specs=(both, both, both, one),
        check_vma=False,
    )
```

```python
import functools

import jax
import jax.numpy as jnp
from jax import lax
from jax.experimental import pallas as pl
from jax.experimental.pallas import tpu as pltpu
from jax.sharding import PartitionSpec as P

AXES = ("clus", "rep")
MIB = 2**20
F32 = jnp.float32
BF16 = jnp.bfloat16
Z1, Z2, CORE, X, Y = 1, 2, 4, 8, 16
ANY = pl.BlockSpec(memory_space=pl.ANY)
SMEM = pl.BlockSpec(memory_space=pltpu.SMEM)
TN = (((0,), (0,)), ((), ()))
NT = (((1,), (1,)), ((), ()))
NN = (((1,), (0,)), ((), ()))
VMEM = pl.BlockSpec(memory_space=pltpu.VMEM)
HBM = pl.BlockSpec(memory_space=pltpu.HBM)
EXTRA = 128


def params(mib=12):
    return pltpu.CompilerParams(vmem_limit_bytes=int(mib * MIB))


def cost(flops, nbytes):
    return pl.CostEstimate(flops=flops, bytes_accessed=nbytes, transcendentals=0)


def column(row):
    return jnp.transpose(jnp.broadcast_to(row, (8, row.shape[1])))[:, :1]


def scale_row(start, degree, count):
    slots = start + lax.broadcasted_iota(jnp.int32, degree.shape, 1)
    live = (slots < count).astype(F32)
    return live / (degree.astype(F32) + 1.0)


def table_kernel(first, ctl, nb, deg, *rest):
    table, ctl_out = rest[-2:]
    hand_on(ctl, ctl_out)
    n = table.shape[0]
    fan, tile = nb.shape
    start = (pl.program_id(0) + first) * tile
    chunk = 256
    used = lax.broadcasted_iota(jnp.int32, (fan, tile), 0) < deg[...]
    slots = jnp.where(used, nb[...], -1)
    targets = lax.broadcasted_iota(jnp.int32, (chunk, tile), 0).astype(F32).astype(BF16)
    own = start + lax.broadcasted_iota(jnp.int32, (1, tile), 1)
    one = jnp.ones((), BF16)
    zero = jnp.zeros((), BF16)

    def local(rows, base):
        off = rows - base
        off = jnp.where(jnp.logical_and(off >= 0, off < chunk), off, -1)
        return off.astype(F32).astype(BF16)

    def build(c, carry):
        base = c * chunk
        here = local(slots, base)
        acc = jnp.where(targets == local(own, base), one + one, zero)
        for k in range(fan):
            acc = acc + jnp.where(targets == here[k : k + 1, :], one, zero)
        table[pl.ds(pl.multiple_of(base, chunk), chunk), :] = acc
        return carry

    lax.fori_loop(0, n // chunk, build, 0)


def neighbour_table(ctl, nb, deg, first, steps, into=None):
    fan, n = nb.shape
    tile = n // 4
    extra = [] if into is None else [into]
    return pl.pallas_call(
        functools.partial(table_kernel, first),
        grid=(steps,),
        in_specs=[
            SMEM,
            pl.BlockSpec((fan, tile), lambda t: (0, t + first)),
            pl.BlockSpec((1, tile), lambda t: (0, t + first)),
        ]
        + [ANY] * len(extra),
        out_specs=[pl.BlockSpec((n, tile), lambda t: (0, t + first)), SMEM],
        out_shape=[pltpu.HBM((n, n), BF16), CTL],
        input_output_aliases={3: 0} if extra else {},
        compiler_params=params(6),
        cost_estimate=cost(n * n * tile * steps, n * tile * steps * 2),
        name="table",
    )(ctl, nb, deg, *extra)


TILE = 256


def scaled(ctl, deg, t, value):
    at = pl.multiple_of(t * TILE, TILE)
    return (value * column(scale_row(at, deg[:, pl.ds(at, TILE)], ctl[1]))).astype(BF16)


CTL = jax.ShapeDtypeStruct((2,), jnp.int32)


def hand_on(ctl, ctl_out):
    ctl_out[0] = ctl[0]
    ctl_out[1] = ctl[1]


def rows_spec(width, first=0):
    return pl.BlockSpec((TILE, width), lambda t: (t + first, 0))


def aggregate_kernel(first, ctl, deg, table, nodes, *rest):
    out, ctl_out, _ = rest[-3:]
    hand_on(ctl, ctl_out)
    t = pl.program_id(0) + first
    value = lax.dot_general(table[...], nodes[...], TN, preferred_element_type=F32)
    out[...] = scaled(ctl, deg, t, value)


def aggregate(ctl, deg, table, nodes, first, steps, into=None):
    n, d = nodes.shape
    extra = [] if into is None else [into]
    return pl.pallas_call(
        functools.partial(aggregate_kernel, first),
        grid=(steps,),
        in_specs=[SMEM, VMEM, pl.BlockSpec((n, TILE), lambda t: (0, t + first)), VMEM] + [ANY] * len(extra),
        out_specs=[rows_spec(d, first), SMEM, ANY],
        out_shape=[pltpu.HBM((n, d), BF16), CTL, pltpu.HBM((n, n), BF16)],
        input_output_aliases={2: 2, 4: 0} if extra else {2: 2},
        compiler_params=params(6.5),
        cost_estimate=cost(2 * steps * TILE * d * n, (n + 2 * steps * TILE) * d * 2),
        name="aggregate",
    )(ctl, deg, table, nodes, *extra)


def halves(ctl, width, far):
    y, x = ctl[0] // 16, lax.rem(ctl[0] // 8, 2)
    if far:
        y, x = 1 - y, 1 - x
    two, four = width // 2, width // 4
    return [(y * two, two)], [(x * four, four), (two + x * four, four)]


def half_product(agg, weight, where, at):
    parts = []
    for start, length in where:
        rows = pl.ds(pl.multiple_of(start, length), length)
        parts.append(jnp.dot(agg[:, rows], weight[rows, at], preferred_element_type=F32))
    return functools.reduce(jnp.add, parts)


def near_kernel(ctl, agg, weight, part, ctl_out, _):
    hand_on(ctl, ctl_out)
    d, m = weight.shape
    for side, where in enumerate(halves(ctl, d, False)):
        at = slice(side * m // 2, (side + 1) * m // 2)
        part[:, at] = half_product(agg, weight, where, at).astype(BF16)


def near_product(ctl, agg, weight):
    n, d = agg.shape
    m = weight.shape[1]
    return pl.pallas_call(
        near_kernel,
        grid=(n // TILE,),
        in_specs=[SMEM, rows_spec(d), VMEM],
        out_specs=[rows_spec(m), SMEM, ANY],
        out_shape=[pltpu.HBM((n, m), BF16), CTL, pltpu.HBM((n, d), BF16)],
        input_output_aliases={1: 2},
        compiler_params=params(8),
        cost_estimate=cost(n * d * m, 8 * n * m),
        name="near",
    )(ctl, agg, weight)


def forward_kernel(split, ctl, agg, weight, bias, cot, *refs):
    act, grad, bias_sum, ctl_out, _ = refs[-5:]
    hand_on(ctl, ctl_out)
    t = pl.program_id(0)
    d, m = weight.shape
    half = m // 2

    @pl.when(t == 0)
    def _():
        bias_sum[...] = jnp.zeros_like(bias_sum)

    slots = t * TILE + lax.broadcasted_iota(jnp.int32, (TILE, half), 0)
    live = (slots < ctl[1]).astype(F32).astype(BF16)
    for side, where in enumerate(halves(ctl, d, True)):
        at = slice(side * half, (side + 1) * half)
        if split:
            pre = half_product(agg, weight, where, at) + refs[0][:, at].astype(F32) + bias[:, at]
        else:
            pre = jnp.dot(agg[...], weight[:, at], preferred_element_type=F32) + bias[:, at]
        sig = jax.nn.sigmoid(pre)
        silu = pre * sig
        act[:, at] = silu.astype(BF16) * live
        slope = (cot[:, at] * live).astype(F32) * (sig + silu * (1.0 - sig))
        grad[:, at] = slope.astype(BF16)
        bias_sum[:, at] += jnp.sum(slope, axis=0, keepdims=True)


def forward(ctl, agg, weight, bias, cot, *part):
    n, d = agg.shape
    m = weight.shape[1]
    return pl.pallas_call(
        functools.partial(forward_kernel, bool(part)),
        grid=(n // TILE,),
        in_specs=[SMEM, rows_spec(d), VMEM, VMEM, rows_spec(m)] + [rows_spec(m)] * len(part),
        out_specs=[rows_spec(m), rows_spec(m), VMEM, SMEM, ANY],
        out_shape=[
            pltpu.HBM((n, m), BF16),
            jax.ShapeDtypeStruct((n, m), BF16),
            jax.ShapeDtypeStruct((1, m), F32),
            CTL,
            pltpu.HBM((n, d), BF16),
        ],
        input_output_aliases={1: 4, 5: 0} if part else {1: 4},
        compiler_params=params(14),
        cost_estimate=cost(2 * n * d * m, 5 * n * m * 2),
        name="forward",
    )(ctl, agg, weight, bias, cot, *part)


def place_kernel(codes, ctl, *refs):
    pieces, refs = refs[: len(codes)], refs[len(codes) :]
    weight, bias, ctl_out, heads, weight_sem, head_sem = refs[-6:]
    hand_on(ctl, ctl_out)
    m = weight.shape[1]
    copies, head_copies, pairs = [], [], []
    for (order, col), piece in zip(codes, pieces):
        rows = piece.shape[0] // len(order)
        wide = min(piece.shape[1], m - col)
        for i, code in enumerate(order):
            owner = lax.bitwise_xor(ctl[0], code)
            copies.append(
                pltpu.make_async_copy(
                    piece.at[pl.ds(i * rows, rows), pl.ds(0, wide)],
                    weight.at[pl.ds(pl.multiple_of(owner * rows, rows), rows), pl.ds(col, wide)],
                    weight_sem.at[len(copies)],
                )
            )
            if wide < piece.shape[1]:
                head = piece.at[pl.ds(i * rows, 16), pl.ds(wide, EXTRA)]
                k = len(head_copies)
                head_copies.append(pltpu.make_async_copy(head, heads.at[k], head_sem.at[k]))
                if code & 1 == 0:
                    pairs.append((k, order.index(code ^ 1) - i + k, owner // 2))
    for c in copies + head_copies:
        c.start()
    bias[...] = refs[1][...] if len(refs) == 8 else jnp.zeros_like(bias)
    for c in head_copies:
        c.wait()
    for one, two, pair in pairs:
        both = heads[one, :1, :].astype(F32) + heads[two, :1, :].astype(F32)
        bias[:, pl.ds(pl.multiple_of(pair * EXTRA, EXTRA), EXTRA)] = both
    for c in copies:
        c.wait()


def place(ctl, pieces, codes, shape, into=()):
    total = sum(len(order) for order, _ in codes)
    first = 1 + len(pieces)
    return pl.pallas_call(
        functools.partial(place_kernel, codes),
        in_specs=[SMEM] + [ANY] * len(pieces) + ([ANY, VMEM] if into else []),
        out_specs=[ANY, VMEM, SMEM],
        out_shape=[jax.ShapeDtypeStruct(shape, BF16), jax.ShapeDtypeStruct((1, shape[1]), F32), CTL],
        input_output_aliases={first: 0} if into else {},
        scratch_shapes=[
            pltpu.VMEM((total // 2, 16, EXTRA), BF16),
            pltpu.SemaphoreType.DMA((total,)),
            pltpu.SemaphoreType.DMA((total // 2,)),
        ],
        compiler_params=params(2),
        cost_estimate=cost(0, 2 * shape[0] * shape[1]),
        name="place",
    )(ctl, *pieces, *into)


def terms_of(me, tile, value, bias_sum, out):
    m = value.shape[1]
    rows = value.shape[0] // 4
    z = lax.rem(me, 4)
    out[:, m:] = jnp.zeros((value.shape[0], EXTRA), BF16)
    head = lax.broadcasted_iota(jnp.int32, (16, EXTRA), 0) == 0
    for q in range(4):
        at = pl.multiple_of(lax.bitwise_xor(z, q) * rows, rows)
        out[pl.ds(at, rows), :m] = value[q * rows : (q + 1) * rows, :].astype(BF16)
        pair = bias_sum[:, pl.ds(pl.multiple_of(tile * TILE + q // 2 * EXTRA, EXTRA), EXTRA)]
        out[pl.ds(at, 16), m:] = jnp.where(head, pair, 0.0).astype(BF16)


def wgrad_kernel(other, ctl, agg, grad, bias_sum, out, ctl_out, _):
    hand_on(ctl, ctl_out)
    tile = lax.bitwise_xor(ctl[0] // 4, 2 * pl.program_id(0) + other)
    value = lax.dot_general(agg[...], grad[...], TN, preferred_element_type=F32)
    terms_of(ctl[0], tile, value, bias_sum, out.at[0])


def wgrad(ctl, agg, grad, bias_sum, other):
    n, d = agg.shape
    m = grad.shape[1]
    return pl.pallas_call(
        functools.partial(wgrad_kernel, other),
        grid_spec=pltpu.PrefetchScalarGridSpec(
            num_scalar_prefetch=1,
            grid=(4,),
            in_specs=[
                pl.BlockSpec((n, TILE), lambda t, ctl: (0, (ctl[0] // 4) ^ (2 * t + other))),
                VMEM,
                VMEM,
            ],
            out_specs=[pl.BlockSpec((1, TILE, m + EXTRA), lambda t, ctl: (t, 0, 0)), SMEM, ANY],
        ),
        out_shape=[jax.ShapeDtypeStruct((4, TILE, m + EXTRA), BF16), CTL, pltpu.HBM((n, d), BF16)],
        input_output_aliases={1: 2},
        compiler_params=params(8),
        cost_estimate=cost(n * d * m, 2 * n * m * 2),
        name="wgrad",
    )(ctl, agg, grad, bias_sum)


def agg_grad_kernel(ctl, deg, grad, weight, out, ctl_out):
    hand_on(ctl, ctl_out)
    value = lax.dot_general(grad[...], weight[...], NT, preferred_element_type=F32)
    out[...] = scaled(ctl, deg, pl.program_id(0), value)


def agg_grad(ctl, deg, grad, weight):
    n, m = grad.shape
    d = weight.shape[0]
    return pl.pallas_call(
        agg_grad_kernel,
        grid=(n // TILE,),
        in_specs=[SMEM, VMEM, rows_spec(m), VMEM],
        out_specs=[rows_spec(d), SMEM],
        out_shape=[jax.ShapeDtypeStruct((n, d), BF16), CTL],
        compiler_params=params(5),
        cost_estimate=cost(2 * n * d * m, 3 * n * m * 2),
        name="agg_grad",
    )(ctl, deg, grad, weight)


def nodes_grad_kernel(ctl, table, spread, *rest):
    out, ctl_out = rest[-2:]
    hand_on(ctl, ctl_out)
    out[...] = jnp.dot(table[...], spread[...], preferred_element_type=F32).astype(BF16)


def nodes_grad(ctl, table, spread, first, steps, into=None):
    n, d = spread.shape
    extra = [] if into is None else [into]
    return pl.pallas_call(
        nodes_grad_kernel,
        grid=(steps,),
        in_specs=[SMEM, rows_spec(n, first), VMEM] + [ANY] * len(extra),
        out_specs=[rows_spec(d, first), SMEM],
        out_shape=[jax.ShapeDtypeStruct((n, d), BF16), CTL],
        input_output_aliases={3: 0} if extra else {},
        compiler_params=params(5),
        cost_estimate=cost(2 * steps * TILE * d * n, (n + 2 * steps * TILE) * d * 2),
        name="nodes_grad",
    )(ctl, table, spread, *extra)


def swap(value, bit):
    return lax.ppermute(value, AXES, [(i, i ^ bit) for i in range(32)])


def after(value, *others):
    return lax.optimization_barrier((value, *others))[0]


def codes_of(*bits):
    order = [0]
    for group in bits:
        order = [code ^ g for g in group for code in order]
    return order


def with_bias(odd, weight, bias):
    rows = bias.shape[0]
    lanes = jnp.concatenate([bias, bias])
    mine = (jnp.arange(EXTRA) >= rows) == odd
    head = jnp.where(mine, lanes, 0).astype(BF16)[None, :]
    tail = jnp.where(jnp.arange(rows)[:, None] == 0, head, 0).astype(BF16)
    return jnp.concatenate([weight, tail], axis=1)


def cat(*parts):
    return jnp.concatenate(parts, axis=0)


def fast(nodes, weight, bias, neighbours, degree, counts, cotangent):
    me = (lax.axis_index("clus") * 4 + lax.axis_index("rep")).astype(jnp.int32)[None]
    ctl = cat(me, counts)
    rows, m = weight.shape
    half = m // 2
    nb = neighbours.T
    deg = degree[None, :]
    steps = nodes.shape[0] // TILE

    odd = me % 2 == 1
    own = with_bias(odd, weight, bias)
    one, two = swap(own, Z1), swap(own, Z2)
    table, ctl = neighbour_table(after(ctl, own), nb, deg, 0, 3)
    one, two = after(one, ctl), after(two, ctl)
    three = swap(two, Z1)
    table, ctl = neighbour_table(after(ctl, two), nb, deg, 3, 1, table)
    three = after(three, ctl)
    p = cat(own[:, :half], one[:, :half], two[:, :half], three[:, :half])
    q = cat(own[:, half:], one[:, half:], two[:, half:], three[:, half:])
    px, qy = swap(p, X), swap(q, Y)
    agg, ctl, table = aggregate(after(ctl, p, q), deg, table, nodes, 0, 3)
    px, qy = after(px, ctl), after(qy, ctl)
    p, q = cat(p, px), cat(q, qy)
    py, qx = swap(p, Y), swap(q, X)
    p_other, q_other = swap(p, CORE), swap(q, CORE)
    agg, ctl, table = aggregate(after(ctl, p, q), deg, table, nodes, 3, steps - 3, agg)
    zs = (0, Z1, Z2, Z1 ^ Z2)
    near_p, near_q = codes_of(zs, (0, X)), codes_of(zs, (0, Y))

    def ends(flip_p, flip_q):
        order_p, order_q = [c ^ flip_p for c in near_p], [c ^ flip_q for c in near_q]
        return (order_p, 0), (order_q, half), ([c ^ CORE for c in order_p], 0), ([c ^ CORE for c in order_q], half)

    *full, ctl = place(ctl, (p, q, p_other, q_other), ends(0, 0), (32 * rows, m))
    part, ctl, agg = near_product(ctl, agg, full[0])
    py, qx = after(py, ctl), after(qx, ctl)
    pieces = (py, qx, swap(py, CORE), swap(qx, CORE))
    full, bias_full, ctl = place(ctl, pieces, ends(Y, X), (32 * rows, m), full)
    act, grad, bias_sum, ctl, agg = forward(ctl, agg, full, bias_full, cotangent, part)

    terms, ctl, agg = wgrad(ctl, agg, grad, bias_sum, 1)
    got = swap(terms, CORE)
    mine, ctl, _ = wgrad(ctl, agg, grad, bias_sum, 0)
    got = after(got, ctl).reshape(2, 2, 4 * rows, m + EXTRA)
    mine = mine.reshape(2, 2, 4 * rows, m + EXTRA)

    def total(*parts):
        return functools.reduce(jnp.add, [part.astype(F32) for part in parts])

    send_p = total(mine[1, :, :, :half], got[1, :, :, :half]).astype(BF16)
    send_q = total(mine[:, 1, :, half:], got[:, 1, :, half:]).astype(BF16)
    got_p, got_q = swap(send_p, Y), swap(send_q, X)
    spread, ctl = agg_grad(after(ctl, send_p, send_q), deg, grad, full)
    got_p, got_q = after(got_p, ctl), after(got_q, ctl)
    next_p = total(mine[0, 1, :, :half], got[0, 1, :, :half], got_p[1]).astype(BF16)
    next_q = total(mine[1, 0, :, half:], got[1, 0, :, half:], got_q[1]).astype(BF16)
    got2_p, got2_q = swap(next_p, X), swap(next_q, Y)
    out, ctl = nodes_grad(after(ctl, next_p, next_q), table, spread, 0, 3)
    got2_p, got2_q = after(got2_p, ctl), after(got2_q, ctl)

    def piece(i):
        at = slice(i * rows, (i + 1) * rows)
        p = total(mine[0, 0, at, :half], got[0, 0, at, :half], got_p[0, at], got2_p[at])
        q = total(mine[0, 0, at, half:], got[0, 0, at, half:], got_q[0, at], got2_q[at])
        return jnp.concatenate([p, q], axis=1)

    third, first = piece(3).astype(BF16), piece(1).astype(BF16)
    far, near = swap(third, Z1), swap(first, Z1)
    out, ctl = nodes_grad(after(ctl, third, first), table, spread, 3, 2, out)
    second = (piece(2) + after(far, ctl).astype(F32)).astype(BF16)
    mid = swap(second, Z2)
    out, ctl = nodes_grad(after(ctl, second), table, spread, 5, steps - 5, out)
    near, mid = after(near, ctl), after(mid, ctl)
    last = piece(0) + near.astype(F32) + mid.astype(F32)
    bias_grad = jnp.where(odd, last[0, m + rows :], last[0, m : m + rows])
    return act, out, last[:, :m], bias_grad


def general(nodes, weight, bias, neighbours, degree, counts, cotangent):
    ctl = cat(jnp.zeros_like(counts), counts)
    nb = neighbours.T
    deg = degree[None, :]
    steps = nodes.shape[0] // TILE
    full = lax.all_gather(weight, AXES, axis=0, tiled=True)
    bias_full = lax.all_gather(bias, AXES, axis=0, tiled=True).astype(F32)[None, :]
    table, _ = neighbour_table(ctl, nb, deg, 0, 4)
    agg, _, table = aggregate(ctl, deg, table, nodes, 0, steps)
    act, grad, bias_sum, _, agg = forward(ctl, agg, full, bias_full, cotangent)
    term = lax.dot_general(agg, grad, TN, preferred_element_type=F32)
    weight_grad = lax.psum_scatter(term, AXES, scatter_dimension=0, tiled=True)
    bias_grad = lax.psum_scatter(bias_sum[0], AXES, scatter_dimension=0, tiled=True)
    spread, _ = agg_grad(ctl, deg, grad, full)
    out, _ = nodes_grad(ctl, table, spread, 0, steps)
    return act, out, weight_grad, bias_grad


def solution(mesh):
    both = P(AXES, None)
    one = P(AXES)
    cube = (mesh.shape["clus"], mesh.shape["rep"]) == (8, 4)
    return jax.shard_map(
        fast if cube else general,
        mesh=mesh,
        in_specs=(both, both, one, both, one, one, both),
        out_specs=(both, both, both, one),
        check_vma=False,
    )
```

```python
import functools

import jax
import jax.numpy as jnp
from jax import lax
from jax.experimental import pallas as pl
from jax.experimental.pallas import tpu as pltpu
from jax.sharding import PartitionSpec as P

AXES = ("clus", "rep")
MIB = 2**20
F32 = jnp.float32
BF16 = jnp.bfloat16
Z1, Z2, CORE, X, Y = 1, 2, 4, 8, 16
ANY = pl.BlockSpec(memory_space=pl.ANY)
SMEM = pl.BlockSpec(memory_space=pltpu.SMEM)
TN = (((0,), (0,)), ((), ()))
NT = (((1,), (1,)), ((), ()))
NN = (((1,), (0,)), ((), ()))
VMEM = pl.BlockSpec(memory_space=pltpu.VMEM)
HBM = pl.BlockSpec(memory_space=pltpu.HBM)
EXTRA = 128


def params(mib=12):
    return pltpu.CompilerParams(vmem_limit_bytes=int(mib * MIB))


def cost(flops, nbytes):
    return pl.CostEstimate(flops=flops, bytes_accessed=nbytes, transcendentals=0)


def column(row):
    return jnp.transpose(jnp.broadcast_to(row, (8, row.shape[1])))[:, :1]


def scale_row(start, degree, count):
    slots = start + lax.broadcasted_iota(jnp.int32, degree.shape, 1)
    live = (slots < count).astype(F32)
    return live / (degree.astype(F32) + 1.0)


def table_kernel(ctl, nb, deg, table, ctl_out):
    hand_on(ctl, ctl_out)
    quarter = table.shape[0] // 4
    fan, tile = nb.shape
    chunk = min(quarter, 128)
    used = lax.broadcasted_iota(jnp.int32, (fan, tile), 0) < deg[...]
    slots = nb[...]
    word = jnp.where(used, slots % quarter, -1)
    value = jnp.left_shift(1, slots // quarter * 8)
    own = pl.program_id(0) * tile + lax.broadcasted_iota(jnp.int32, (1, tile), 1)
    own_word, own_value = own % quarter, jnp.left_shift(2, own // quarter * 8)
    words = lax.broadcasted_iota(jnp.int32, (chunk, tile), 0)

    def build(c, carry):
        base = c * chunk
        at = words + base
        acc = jnp.where(at == own_word, own_value, 0)
        for k in range(fan):
            acc = acc + jnp.where(at == word[k : k + 1, :], value[k : k + 1, :], 0)
        for part in range(4):
            counts = jnp.bitwise_and(jnp.right_shift(acc, 8 * part), 255)
            rows = pl.ds(pl.multiple_of(part * quarter + base, chunk), chunk)
            table[rows, :] = counts.astype(F32).astype(BF16)
        return carry

    lax.fori_loop(0, quarter // chunk, build, 0)


def neighbour_table(ctl, nb, deg):
    fan, n = nb.shape
    return pl.pallas_call(
        table_kernel,
        grid=(n // TILE,),
        in_specs=[
            SMEM,
            pl.BlockSpec((fan, TILE), lambda t: (0, t)),
            pl.BlockSpec((1, TILE), lambda t: (0, t)),
        ],
        out_specs=[pl.BlockSpec((n, TILE), lambda t: (0, t)), SMEM],
        out_shape=[pltpu.HBM((n, n), BF16), CTL],
        compiler_params=params(6),
        cost_estimate=cost(n * n * n, n * n * 2),
        name="table",
    )(ctl, nb, deg)


TILE = 256


def scaled(ctl, deg, t, value):
    at = pl.multiple_of(t * TILE, TILE)
    return (value * column(scale_row(at, deg[:, pl.ds(at, TILE)], ctl[1]))).astype(BF16)


CTL = jax.ShapeDtypeStruct((2,), jnp.int32)


def hand_on(ctl, ctl_out):
    ctl_out[0] = ctl[0]
    ctl_out[1] = ctl[1]


def rows_spec(width, first=0):
    return pl.BlockSpec((TILE, width), lambda t: (t + first, 0))


def aggregate_kernel(first, ctl, deg, table, nodes, *rest):
    out, ctl_out, _ = rest[-3:]
    hand_on(ctl, ctl_out)
    t = pl.program_id(0) + first
    value = lax.dot_general(table[...], nodes[...], TN, preferred_element_type=F32)
    out[...] = scaled(ctl, deg, t, value)


def aggregate(ctl, deg, table, nodes, first, steps, into=None):
    n, d = nodes.shape
    extra = [] if into is None else [into]
    return pl.pallas_call(
        functools.partial(aggregate_kernel, first),
        grid=(steps,),
        in_specs=[SMEM, VMEM, pl.BlockSpec((n, TILE), lambda t: (0, t + first)), VMEM] + [ANY] * len(extra),
        out_specs=[rows_spec(d, first), SMEM, ANY],
        out_shape=[pltpu.HBM((n, d), BF16), CTL, pltpu.HBM((n, n), BF16)],
        input_output_aliases={2: 2, 4: 0} if extra else {2: 2},
        compiler_params=params(6.5),
        cost_estimate=cost(2 * steps * TILE * d * n, (n + 2 * steps * TILE) * d * 2),
        name="aggregate",
    )(ctl, deg, table, nodes, *extra)


def halves(ctl, width, far):
    y, x = ctl[0] // 16, lax.rem(ctl[0] // 8, 2)
    if far:
        y, x = 1 - y, 1 - x
    two, four = width // 2, width // 4
    return [(y * two, two)], [(x * four, four), (two + x * four, four)]


def half_product(agg, weight, where, at):
    parts = []
    for start, length in where:
        rows = pl.ds(pl.multiple_of(start, length), length)
        parts.append(jnp.dot(agg[:, rows], weight[rows, at], preferred_element_type=F32))
    return functools.reduce(jnp.add, parts)


def near_kernel(ctl, agg, weight, part, ctl_out, _):
    hand_on(ctl, ctl_out)
    d, m = weight.shape
    for side, where in enumerate(halves(ctl, d, False)):
        at = slice(side * m // 2, (side + 1) * m // 2)
        part[:, at] = half_product(agg, weight, where, at).astype(BF16)


def near_product(ctl, agg, weight):
    n, d = agg.shape
    m = weight.shape[1]
    return pl.pallas_call(
        near_kernel,
        grid=(n // TILE,),
        in_specs=[SMEM, rows_spec(d), VMEM],
        out_specs=[rows_spec(m), SMEM, ANY],
        out_shape=[pltpu.HBM((n, m), BF16), CTL, pltpu.HBM((n, d), BF16)],
        input_output_aliases={1: 2},
        compiler_params=params(8),
        cost_estimate=cost(n * d * m, 8 * n * m),
        name="near",
    )(ctl, agg, weight)


def forward_kernel(split, ctl, agg, weight, bias, cot, *refs):
    act, grad, bias_sum, ctl_out, _ = refs[-5:]
    hand_on(ctl, ctl_out)
    t = pl.program_id(0)
    d, m = weight.shape
    half = m // 2

    @pl.when(t == 0)
    def _():
        bias_sum[...] = jnp.zeros_like(bias_sum)

    slots = t * TILE + lax.broadcasted_iota(jnp.int32, (TILE, half), 0)
    live = (slots < ctl[1]).astype(F32).astype(BF16)
    for side, where in enumerate(halves(ctl, d, True)):
        at = slice(side * half, (side + 1) * half)
        if split:
            pre = half_product(agg, weight, where, at) + refs[0][:, at].astype(F32) + bias[:, at]
        else:
            pre = jnp.dot(agg[...], weight[:, at], preferred_element_type=F32) + bias[:, at]
        sig = jax.nn.sigmoid(pre)
        silu = pre * sig
        act[:, at] = silu.astype(BF16) * live
        slope = (cot[:, at] * live).astype(F32) * (sig + silu * (1.0 - sig))
        grad[:, at] = slope.astype(BF16)
        bias_sum[:, at] += jnp.sum(slope, axis=0, keepdims=True)


def forward(ctl, agg, weight, bias, cot, *part):
    n, d = agg.shape
    m = weight.shape[1]
    return pl.pallas_call(
        functools.partial(forward_kernel, bool(part)),
        grid=(n // TILE,),
        in_specs=[SMEM, rows_spec(d), VMEM, VMEM, rows_spec(m)] + [rows_spec(m)] * len(part),
        out_specs=[rows_spec(m), rows_spec(m), VMEM, SMEM, ANY],
        out_shape=[
            pltpu.HBM((n, m), BF16),
            jax.ShapeDtypeStruct((n, m), BF16),
            jax.ShapeDtypeStruct((1, m), F32),
            CTL,
            pltpu.HBM((n, d), BF16),
        ],
        input_output_aliases={1: 4, 5: 0} if part else {1: 4},
        compiler_params=params(14),
        cost_estimate=cost(2 * n * d * m, 5 * n * m * 2),
        name="forward",
    )(ctl, agg, weight, bias, cot, *part)


def place_kernel(codes, ctl, *refs):
    pieces, refs = refs[: len(codes)], refs[len(codes) :]
    weight, bias, ctl_out, heads, weight_sem, head_sem = refs[-6:]
    hand_on(ctl, ctl_out)
    m = weight.shape[1]
    copies, head_copies, pairs = [], [], []
    for (order, col), piece in zip(codes, pieces):
        rows = piece.shape[0] // len(order)
        wide = min(piece.shape[1], m - col)
        for i, code in enumerate(order):
            owner = lax.bitwise_xor(ctl[0], code)
            copies.append(
                pltpu.make_async_copy(
                    piece.at[pl.ds(i * rows, rows), pl.ds(0, wide)],
                    weight.at[pl.ds(pl.multiple_of(owner * rows, rows), rows), pl.ds(col, wide)],
                    weight_sem.at[len(copies)],
                )
            )
            if wide < piece.shape[1]:
                head = piece.at[pl.ds(i * rows, 16), pl.ds(wide, EXTRA)]
                k = len(head_copies)
                head_copies.append(pltpu.make_async_copy(head, heads.at[k], head_sem.at[k]))
                if code & 1 == 0:
                    pairs.append((k, order.index(code ^ 1) - i + k, owner // 2))
    for c in copies + head_copies:
        c.start()
    bias[...] = refs[1][...] if len(refs) == 8 else jnp.zeros_like(bias)
    for c in head_copies:
        c.wait()
    for one, two, pair in pairs:
        both = heads[one, :1, :].astype(F32) + heads[two, :1, :].astype(F32)
        bias[:, pl.ds(pl.multiple_of(pair * EXTRA, EXTRA), EXTRA)] = both
    for c in copies:
        c.wait()


def place(ctl, pieces, codes, shape, into=()):
    total = sum(len(order) for order, _ in codes)
    first = 1 + len(pieces)
    return pl.pallas_call(
        functools.partial(place_kernel, codes),
        in_specs=[SMEM] + [ANY] * len(pieces) + ([ANY, VMEM] if into else []),
        out_specs=[ANY, VMEM, SMEM],
        out_shape=[jax.ShapeDtypeStruct(shape, BF16), jax.ShapeDtypeStruct((1, shape[1]), F32), CTL],
        input_output_aliases={first: 0} if into else {},
        scratch_shapes=[
            pltpu.VMEM((total // 2, 16, EXTRA), BF16),
            pltpu.SemaphoreType.DMA((total,)),
            pltpu.SemaphoreType.DMA((total // 2,)),
        ],
        compiler_params=params(2),
        cost_estimate=cost(0, 2 * shape[0] * shape[1]),
        name="place",
    )(ctl, *pieces, *into)


def terms_of(me, tile, value, bias_sum, out):
    m = value.shape[1]
    rows = value.shape[0] // 4
    z = lax.rem(me, 4)
    out[:, m:] = jnp.zeros((value.shape[0], EXTRA), BF16)
    head = lax.broadcasted_iota(jnp.int32, (16, EXTRA), 0) == 0
    for q in range(4):
        at = pl.multiple_of(lax.bitwise_xor(z, q) * rows, rows)
        out[pl.ds(at, rows), :m] = value[q * rows : (q + 1) * rows, :].astype(BF16)
        pair = bias_sum[:, pl.ds(pl.multiple_of(tile * TILE + q // 2 * EXTRA, EXTRA), EXTRA)]
        out[pl.ds(at, 16), m:] = jnp.where(head, pair, 0.0).astype(BF16)


def wgrad_kernel(code, ctl, agg, grad, bias_sum, out, ctl_out, _):
    hand_on(ctl, ctl_out)
    tile = lax.bitwise_xor(ctl[0] // 4, 2 * pl.program_id(0) + code)
    value = lax.dot_general(agg[...], grad[...], TN, preferred_element_type=F32)
    terms_of(ctl[0], tile, value, bias_sum, out.at[0])


def wgrad(ctl, agg, grad, bias_sum, code, steps):
    n, d = agg.shape
    m = grad.shape[1]
    return pl.pallas_call(
        functools.partial(wgrad_kernel, code),
        grid_spec=pltpu.PrefetchScalarGridSpec(
            num_scalar_prefetch=1,
            grid=(steps,),
            in_specs=[
                pl.BlockSpec((n, TILE), lambda t, ctl: (0, (ctl[0] // 4) ^ (2 * t + code))),
                VMEM,
                VMEM,
            ],
            out_specs=[pl.BlockSpec((1, TILE, m + EXTRA), lambda t, ctl: (t, 0, 0)), SMEM, ANY],
        ),
        out_shape=[jax.ShapeDtypeStruct((steps, TILE, m + EXTRA), BF16), CTL, pltpu.HBM((n, d), BF16)],
        input_output_aliases={1: 2},
        compiler_params=params(8),
        cost_estimate=cost(2 * n * TILE * steps * m, 2 * n * m * 2),
        name="wgrad",
    )(ctl, agg, grad, bias_sum)


def agg_grad_kernel(ctl, deg, grad, weight, out, ctl_out):
    hand_on(ctl, ctl_out)
    value = lax.dot_general(grad[...], weight[...], NT, preferred_element_type=F32)
    out[...] = scaled(ctl, deg, pl.program_id(0), value)


def agg_grad(ctl, deg, grad, weight):
    n, m = grad.shape
    d = weight.shape[0]
    return pl.pallas_call(
        agg_grad_kernel,
        grid=(n // TILE,),
        in_specs=[SMEM, VMEM, rows_spec(m), VMEM],
        out_specs=[rows_spec(d), SMEM],
        out_shape=[jax.ShapeDtypeStruct((n, d), BF16), CTL],
        compiler_params=params(5),
        cost_estimate=cost(2 * n * d * m, 3 * n * m * 2),
        name="agg_grad",
    )(ctl, deg, grad, weight)


def nodes_grad_kernel(ctl, table, spread, *rest):
    out, ctl_out = rest[-2:]
    hand_on(ctl, ctl_out)
    out[...] = jnp.dot(table[...], spread[...], preferred_element_type=F32).astype(BF16)


def nodes_grad(ctl, table, spread, first, steps, into=None):
    n, d = spread.shape
    extra = [] if into is None else [into]
    return pl.pallas_call(
        nodes_grad_kernel,
        grid=(steps,),
        in_specs=[SMEM, rows_spec(n, first), VMEM] + [ANY] * len(extra),
        out_specs=[rows_spec(d, first), SMEM],
        out_shape=[jax.ShapeDtypeStruct((n, d), BF16), CTL],
        input_output_aliases={3: 0} if extra else {},
        compiler_params=params(5),
        cost_estimate=cost(2 * steps * TILE * d * n, (n + 2 * steps * TILE) * d * 2),
        name="nodes_grad",
    )(ctl, table, spread, *extra)


def swap(value, bit):
    return lax.ppermute(value, AXES, [(i, i ^ bit) for i in range(32)])


def after(value, *others):
    return lax.optimization_barrier((value, *others))[0]


def codes_of(*bits):
    order = [0]
    for group in bits:
        order = [code ^ g for g in group for code in order]
    return order


def with_bias(odd, weight, bias):
    rows = bias.shape[0]
    lanes = jnp.concatenate([bias, bias])
    mine = (jnp.arange(EXTRA) >= rows) == odd
    head = jnp.where(mine, lanes, 0).astype(BF16)[None, :]
    tail = jnp.where(jnp.arange(rows)[:, None] == 0, head, 0).astype(BF16)
    return jnp.concatenate([weight, tail], axis=1)


def cat(*parts):
    return jnp.concatenate(parts, axis=0)


def fast(nodes, weight, bias, neighbours, degree, counts, cotangent):
    me = (lax.axis_index("clus") * 4 + lax.axis_index("rep")).astype(jnp.int32)[None]
    ctl = cat(me, counts)
    rows, m = weight.shape
    half = m // 2
    nb = neighbours.T
    deg = degree[None, :]
    steps = nodes.shape[0] // TILE

    odd = me % 2 == 1
    own = with_bias(odd, weight, bias)
    one, two = swap(own, Z1), swap(own, Z2)
    table, ctl = neighbour_table(after(ctl, own), nb, deg)
    one, two = after(one, ctl), after(two, ctl)
    three = swap(two, Z1)
    agg, ctl, table = aggregate(after(ctl, two), deg, table, nodes, 0, 2)
    three = after(three, ctl)
    p = cat(own[:, :half], one[:, :half], two[:, :half], three[:, :half])
    q = cat(own[:, half:], one[:, half:], two[:, half:], three[:, half:])
    px, qy = swap(p, X), swap(q, Y)
    agg, ctl, table = aggregate(after(ctl, p, q), deg, table, nodes, 2, 4, agg)
    px, qy = after(px, ctl), after(qy, ctl)
    p, q = cat(p, px), cat(q, qy)
    py, qx = swap(p, Y), swap(q, X)
    p_other, q_other = swap(p, CORE), swap(q, CORE)
    agg, ctl, table = aggregate(after(ctl, p, q), deg, table, nodes, 6, steps - 6, agg)
    zs = (0, Z1, Z2, Z1 ^ Z2)
    near_p, near_q = codes_of(zs, (0, X)), codes_of(zs, (0, Y))

    def ends(flip_p, flip_q):
        order_p, order_q = [c ^ flip_p for c in near_p], [c ^ flip_q for c in near_q]
        return (order_p, 0), (order_q, half), ([c ^ CORE for c in order_p], 0), ([c ^ CORE for c in order_q], half)

    *full, ctl = place(ctl, (p, q, p_other, q_other), ends(0, 0), (32 * rows, m))
    part, ctl, agg = near_product(ctl, agg, full[0])
    py, qx = after(py, ctl), after(qx, ctl)
    pieces = (py, qx, swap(py, CORE), swap(qx, CORE))
    full, bias_full, ctl = place(ctl, pieces, ends(Y, X), (32 * rows, m), full)
    act, grad, bias_sum, ctl, agg = forward(ctl, agg, full, bias_full, cotangent, part)

    terms, ctl, agg = wgrad(ctl, agg, grad, bias_sum, 1, 4)
    got = swap(terms, CORE)
    mine, ctl, agg = wgrad(ctl, agg, grad, bias_sum, 2, 3)
    got = after(got, ctl)

    def total(*parts):
        return functools.reduce(jnp.add, [part.astype(F32) for part in parts])

    send_p = total(mine[1:, :, :half], got[2:, :, :half]).astype(BF16)
    send_q = total(mine[::2, :, half:], got[1::2, :, half:]).astype(BF16)
    got_p, got_q = swap(send_p, Y), swap(send_q, X)
    kept, ctl, _ = wgrad(after(ctl, send_p, send_q), agg, grad, bias_sum, 0, 1)
    spread, ctl = agg_grad(ctl, deg, grad, full)
    got_p, got_q = after(got_p, ctl), after(got_q, ctl)
    next_p = total(mine[0, :, :half], got[1, :, :half], got_p[1]).astype(BF16)
    next_q = total(mine[1, :, half:], got[2, :, half:], got_q[1]).astype(BF16)
    got2_p, got2_q = swap(next_p, X), swap(next_q, Y)
    out, ctl = nodes_grad(after(ctl, next_p, next_q), table, spread, 0, 3)
    got2_p, got2_q = after(got2_p, ctl), after(got2_q, ctl)

    def piece(i):
        at = slice(i * rows, (i + 1) * rows)
        p = total(kept[0, at, :half], got[0, at, :half], got_p[0, at], got2_p[at])
        q = total(kept[0, at, half:], got[0, at, half:], got_q[0, at], got2_q[at])
        return jnp.concatenate([p, q], axis=1)

    third, first = piece(3).astype(BF16), piece(1).astype(BF16)
    far = swap(third, Z1)
    out, ctl = nodes_grad(after(ctl, third, first), table, spread, 3, 2, out)
    far = after(far, ctl)
    second = (piece(2) + far.astype(F32)).astype(BF16)
    mid, near = swap(second, Z2), swap(after(first, far), Z1)
    out, ctl = nodes_grad(after(ctl, second), table, spread, 5, steps - 5, out)
    near, mid = after(near, ctl), after(mid, ctl)
    own_rows = piece(0)
    weight_grad = total(own_rows[:, :m], near[:, :m], mid[:, :m])
    ends = total(own_rows[0, m:], near[0, m:], mid[0, m:])
    return act, out, weight_grad, jnp.where(odd, ends[rows:], ends[:rows])


def general(nodes, weight, bias, neighbours, degree, counts, cotangent):
    ctl = cat(jnp.zeros_like(counts), counts)
    nb = neighbours.T
    deg = degree[None, :]
    steps = nodes.shape[0] // TILE
    full = lax.all_gather(weight, AXES, axis=0, tiled=True)
    bias_full = lax.all_gather(bias, AXES, axis=0, tiled=True).astype(F32)[None, :]
    table, _ = neighbour_table(ctl, nb, deg)
    agg, _, table = aggregate(ctl, deg, table, nodes, 0, steps)
    act, grad, bias_sum, _, agg = forward(ctl, agg, full, bias_full, cotangent)
    term = lax.dot_general(agg, grad, TN, preferred_element_type=F32)
    weight_grad = lax.psum_scatter(term, AXES, scatter_dimension=0, tiled=True)
    bias_grad = lax.psum_scatter(bias_sum[0], AXES, scatter_dimension=0, tiled=True)
    spread, _ = agg_grad(ctl, deg, grad, full)
    out, _ = nodes_grad(ctl, table, spread, 0, steps)
    return act, out, weight_grad, bias_grad


def solution(mesh):
    both = P(AXES, None)
    one = P(AXES)
    cube = (mesh.shape["clus"], mesh.shape["rep"]) == (8, 4)
    return jax.shard_map(
        fast if cube else general,
        mesh=mesh,
        in_specs=(both, both, one, both, one, one, both),
        out_specs=(both, both, both, one),
        check_vma=False,
    )
```

```python
import functools

import jax
import jax.numpy as jnp
from jax import lax
from jax.experimental import pallas as pl
from jax.experimental.pallas import tpu as pltpu
from jax.sharding import PartitionSpec as P

AXES = ("clus", "rep")
MIB = 2**20
F32 = jnp.float32
BF16 = jnp.bfloat16
Z1, Z2, CORE, X, Y = 1, 2, 4, 8, 16
ANY = pl.BlockSpec(memory_space=pl.ANY)
SMEM = pl.BlockSpec(memory_space=pltpu.SMEM)
TN = (((0,), (0,)), ((), ()))
NT = (((1,), (1,)), ((), ()))
NN = (((1,), (0,)), ((), ()))
VMEM = pl.BlockSpec(memory_space=pltpu.VMEM)
HBM = pl.BlockSpec(memory_space=pltpu.HBM)
EXTRA = 128
HEAD = 16


def params(mib=12):
    return pltpu.CompilerParams(vmem_limit_bytes=int(mib * MIB))


def cost(flops, nbytes):
    return pl.CostEstimate(flops=flops, bytes_accessed=nbytes, transcendentals=0)


def column(row):
    return jnp.transpose(jnp.broadcast_to(row, (8, row.shape[1])))[:, :1]


def scale_row(start, degree, count):
    slots = start + lax.broadcasted_iota(jnp.int32, degree.shape, 1)
    live = (slots < count).astype(F32)
    return live / (degree.astype(F32) + 1.0)


def table_kernel(ctl, used, table, ctl_out):
    hand_on(ctl, ctl_out)
    quarter = table.shape[0] // 4
    fan, tile = used.shape
    chunk = min(quarter, 128)
    slots = used[...]
    word = jnp.where(slots >= 0, slots % quarter, -1)
    value = jnp.left_shift(1, jnp.maximum(slots, 0) // quarter * 8)
    own = pl.program_id(0) * tile + lax.broadcasted_iota(jnp.int32, (1, tile), 1)
    own_word, own_value = own % quarter, jnp.left_shift(2, own // quarter * 8)
    words = lax.broadcasted_iota(jnp.int32, (chunk, tile), 0)

    def build(c, carry):
        base = c * chunk
        at = words + base
        acc = jnp.where(at == own_word, own_value, 0)
        for k in range(fan):
            acc = acc + jnp.where(at == word[k : k + 1, :], value[k : k + 1, :], 0)
        for part in range(4):
            counts = jnp.bitwise_and(jnp.right_shift(acc, 8 * part), 255)
            rows = pl.ds(pl.multiple_of(part * quarter + base, chunk), chunk)
            table[rows, :] = counts.astype(F32).astype(BF16)
        return carry

    lax.fori_loop(0, quarter // chunk, build, 0)


def neighbour_table(ctl, nb, deg):
    fan, n = nb.shape
    used = jnp.where(jnp.arange(fan, dtype=jnp.int32)[:, None] < deg, nb, -1)
    return pl.pallas_call(
        table_kernel,
        grid=(n // TILE,),
        in_specs=[
            SMEM,
            pl.BlockSpec((fan, TILE), lambda t: (0, t)),
        ],
        out_specs=[pl.BlockSpec((n, TILE), lambda t: (0, t)), SMEM],
        out_shape=[pltpu.HBM((n, n), BF16), CTL],
        compiler_params=params(6),
        cost_estimate=cost(n * n * n, n * n * 2),
        name="table",
    )(ctl, used)


TILE = 256


def scaled(ctl, deg, t, value):
    at = pl.multiple_of(t * TILE, TILE)
    return (value * column(scale_row(at, deg[:, pl.ds(at, TILE)], ctl[1]))).astype(BF16)


CTL = jax.ShapeDtypeStruct((2,), jnp.int32)


def hand_on(ctl, ctl_out):
    ctl_out[0] = ctl[0]
    ctl_out[1] = ctl[1]


def rows_spec(width, first=0):
    return pl.BlockSpec((TILE, width), lambda t: (t + first, 0))


def aggregate_kernel(first, ctl, deg, table, nodes, *rest):
    out, ctl_out, _ = rest[-3:]
    hand_on(ctl, ctl_out)
    t = pl.program_id(0) + first
    value = lax.dot_general(table[...], nodes[...], TN, preferred_element_type=F32)
    out[...] = scaled(ctl, deg, t, value)


def aggregate(ctl, deg, table, nodes, first, steps, into=None):
    n, d = nodes.shape
    extra = [] if into is None else [into]
    return pl.pallas_call(
        functools.partial(aggregate_kernel, first),
        grid=(steps,),
        in_specs=[SMEM, VMEM, pl.BlockSpec((n, TILE), lambda t: (0, t + first)), VMEM] + [ANY] * len(extra),
        out_specs=[rows_spec(d, first), SMEM, ANY],
        out_shape=[pltpu.HBM((n, d), BF16), CTL, pltpu.HBM((n, n), BF16)],
        input_output_aliases={2: 2, 4: 0} if extra else {2: 2},
        compiler_params=params(6.5),
        cost_estimate=cost(2 * steps * TILE * d * n, (n + 2 * steps * TILE) * d * 2),
        name="aggregate",
    )(ctl, deg, table, nodes, *extra)


def halves(ctl, width, far):
    y, x = ctl[0] // 16, lax.rem(ctl[0] // 8, 2)
    if far:
        y, x = 1 - y, 1 - x
    two, four = width // 2, width // 4
    return [(y * two, two)], [(x * four, four), (two + x * four, four)]


def half_product(agg, weight, where, at):
    parts = []
    for start, length in where:
        rows = pl.ds(pl.multiple_of(start, length), length)
        parts.append(jnp.dot(agg[:, rows], weight[rows, at], preferred_element_type=F32))
    return functools.reduce(jnp.add, parts)


def near_kernel(ctl, agg, weight, part, ctl_out, _):
    hand_on(ctl, ctl_out)
    d, m = weight.shape
    for side, where in enumerate(halves(ctl, d, False)):
        at = slice(side * m // 2, (side + 1) * m // 2)
        part[:, at] = half_product(agg, weight, where, at).astype(BF16)


def near_product(ctl, agg, weight):
    n, d = agg.shape
    m = weight.shape[1]
    return pl.pallas_call(
        near_kernel,
        grid=(n // TILE,),
        in_specs=[SMEM, rows_spec(d), VMEM],
        out_specs=[rows_spec(m), SMEM, ANY],
        out_shape=[pltpu.HBM((n, m), BF16), CTL, pltpu.HBM((n, d), BF16)],
        input_output_aliases={1: 2},
        compiler_params=params(8),
        cost_estimate=cost(n * d * m, 8 * n * m),
        name="near",
    )(ctl, agg, weight)


def forward_kernel(split, ctl, agg, weight, bias, cot, *refs):
    act, grad, bias_sum, ctl_out, _ = refs[-5:]
    hand_on(ctl, ctl_out)
    t = pl.program_id(0)
    d, m = weight.shape
    half = m // 2

    @pl.when(t == 0)
    def _():
        bias_sum[...] = jnp.zeros_like(bias_sum)

    slots = t * TILE + lax.broadcasted_iota(jnp.int32, (TILE, half), 0)
    live = (slots < ctl[1]).astype(F32).astype(BF16)
    for side, where in enumerate(halves(ctl, d, True)):
        at = slice(side * half, (side + 1) * half)
        if split:
            pre = half_product(agg, weight, where, at) + refs[0][:, at].astype(F32) + bias[:, at]
        else:
            pre = jnp.dot(agg[...], weight[:, at], preferred_element_type=F32) + bias[:, at]
        sig = jax.nn.sigmoid(pre)
        silu = pre * sig
        act[:, at] = silu.astype(BF16) * live
        slope = (cot[:, at] * live).astype(F32) * (sig + silu * (1.0 - sig))
        grad[:, at] = slope.astype(BF16)
        bias_sum[:, at] += jnp.sum(slope, axis=0, keepdims=True)


def forward(ctl, agg, weight, bias, cot, *part):
    n, d = agg.shape
    m = weight.shape[1]
    return pl.pallas_call(
        functools.partial(forward_kernel, bool(part)),
        grid=(n // TILE,),
        in_specs=[SMEM, rows_spec(d), VMEM, VMEM, rows_spec(m)] + [rows_spec(m)] * len(part),
        out_specs=[rows_spec(m), rows_spec(m), VMEM, SMEM, ANY],
        out_shape=[
            pltpu.HBM((n, m), BF16),
            jax.ShapeDtypeStruct((n, m), BF16),
            jax.ShapeDtypeStruct((1, m), F32),
            CTL,
            pltpu.HBM((n, d), BF16),
        ],
        input_output_aliases={1: 4, 5: 0} if part else {1: 4},
        compiler_params=params(14),
        cost_estimate=cost(2 * n * d * m, 5 * n * m * 2),
        name="forward",
    )(ctl, agg, weight, bias, cot, *part)


def place_kernel(codes, ctl, *refs):
    pieces, refs = refs[: len(codes)], refs[len(codes) :]
    weight, bias, ctl_out, heads, weight_sem, head_sem = refs[-6:]
    hand_on(ctl, ctl_out)
    half = weight.shape[1] // 2
    rows = weight.shape[0] // 32
    copies, head_copies, pairs = [], [], []
    for (order, col, headed), piece in zip(codes, pieces):
        group = 4 * rows + HEAD * headed
        for i, code in enumerate(order):
            owner = lax.bitwise_xor(ctl[0], code)
            start = i // 4 * group + i % 4 * rows
            copies.append(
                pltpu.make_async_copy(
                    piece.at[pl.ds(start, rows), :],
                    weight.at[pl.ds(pl.multiple_of(owner * rows, rows), rows), pl.ds(col, half)],
                    weight_sem.at[len(copies)],
                )
            )
            if headed and i % 4 == 0:
                k = len(head_copies)
                head = piece.at[pl.ds(start + 4 * rows, HEAD), pl.ds(0, 4 * EXTRA)]
                head_copies.append(pltpu.make_async_copy(head, heads.at[k], head_sem.at[k]))
            if headed and i % 2 == 0:
                pairs.append((i % 4 * EXTRA, len(head_copies) - 1, owner // 2))
    for c in copies + head_copies:
        c.start()
    bias[...] = refs[1][...] if len(refs) == 8 else jnp.zeros_like(bias)
    for c in head_copies:
        c.wait()
    for lane, k, pair in pairs:
        one = heads[k, :1, lane : lane + EXTRA].astype(F32)
        two = heads[k, :1, lane + EXTRA : lane + 2 * EXTRA].astype(F32)
        bias[:, pl.ds(pl.multiple_of(pair * EXTRA, EXTRA), EXTRA)] = one + two
    for c in copies:
        c.wait()


def place(ctl, pieces, codes, shape, into=()):
    total = sum(len(order) for order, _, _ in codes)
    first = 1 + len(pieces)
    return pl.pallas_call(
        functools.partial(place_kernel, codes),
        in_specs=[SMEM] + [ANY] * len(pieces) + ([ANY, VMEM] if into else []),
        out_specs=[ANY, VMEM, SMEM],
        out_shape=[jax.ShapeDtypeStruct(shape, BF16), jax.ShapeDtypeStruct((1, shape[1]), F32), CTL],
        input_output_aliases={first: 0} if into else {},
        scratch_shapes=[
            pltpu.VMEM((total // 8, HEAD, 4 * EXTRA), BF16),
            pltpu.SemaphoreType.DMA((total,)),
            pltpu.SemaphoreType.DMA((total // 8,)),
        ],
        compiler_params=params(2),
        cost_estimate=cost(0, 2 * shape[0] * shape[1]),
        name="place",
    )(ctl, *pieces, *into)


def terms_of(me, tile, value, bias_sum, out):
    count, m = value.shape
    rows = count // 4
    z = lax.rem(me, 4)
    out[count:, :] = jnp.zeros((HEAD, m), BF16)
    top = lax.broadcasted_iota(jnp.int32, (HEAD, EXTRA), 0) == 0
    for q in range(4):
        place = lax.bitwise_xor(z, q)
        out[pl.ds(pl.multiple_of(place * rows, rows), rows), :] = value[q * rows : (q + 1) * rows, :].astype(BF16)
        pair = bias_sum[:, pl.ds(pl.multiple_of(tile * TILE + q // 2 * EXTRA, EXTRA), EXTRA)]
        out[count:, pl.ds(pl.multiple_of(place * EXTRA, EXTRA), EXTRA)] = jnp.where(top, pair, 0.0).astype(BF16)


def wgrad_kernel(code, ctl, agg, grad, bias_sum, out, ctl_out, _):
    hand_on(ctl, ctl_out)
    tile = lax.bitwise_xor(ctl[0] // 4, 2 * pl.program_id(0) + code)
    value = lax.dot_general(agg[...], grad[...], TN, preferred_element_type=F32)
    terms_of(ctl[0], tile, value, bias_sum, out.at[0])


def wgrad(ctl, agg, grad, bias_sum, code, steps):
    n, d = agg.shape
    m = grad.shape[1]
    return pl.pallas_call(
        functools.partial(wgrad_kernel, code),
        grid_spec=pltpu.PrefetchScalarGridSpec(
            num_scalar_prefetch=1,
            grid=(steps,),
            in_specs=[
                pl.BlockSpec((n, TILE), lambda t, ctl: (0, (ctl[0] // 4) ^ (2 * t + code))),
                VMEM,
                VMEM,
            ],
            out_specs=[pl.BlockSpec((1, TILE + HEAD, m), lambda t, ctl: (t, 0, 0)), SMEM, ANY],
        ),
        out_shape=[jax.ShapeDtypeStruct((steps, TILE + HEAD, m), BF16), CTL, pltpu.HBM((n, d), BF16)],
        input_output_aliases={1: 2},
        compiler_params=params(8),
        cost_estimate=cost(2 * n * TILE * steps * m, 2 * n * m * 2),
        name="wgrad",
    )(ctl, agg, grad, bias_sum)


def agg_grad_kernel(ctl, deg, grad, weight, out, ctl_out):
    hand_on(ctl, ctl_out)
    value = lax.dot_general(grad[...], weight[...], NT, preferred_element_type=F32)
    out[...] = scaled(ctl, deg, pl.program_id(0), value)


def agg_grad(ctl, deg, grad, weight):
    n, m = grad.shape
    d = weight.shape[0]
    return pl.pallas_call(
        agg_grad_kernel,
        grid=(n // TILE,),
        in_specs=[SMEM, VMEM, rows_spec(m), VMEM],
        out_specs=[rows_spec(d), SMEM],
        out_shape=[jax.ShapeDtypeStruct((n, d), BF16), CTL],
        compiler_params=params(5),
        cost_estimate=cost(2 * n * d * m, 3 * n * m * 2),
        name="agg_grad",
    )(ctl, deg, grad, weight)


def nodes_grad_kernel(ctl, table, spread, *rest):
    out, ctl_out = rest[-2:]
    hand_on(ctl, ctl_out)
    out[...] = jnp.dot(table[...], spread[...], preferred_element_type=F32).astype(BF16)


def nodes_grad(ctl, table, spread, first, steps, into=None, behind=()):
    n, d = spread.shape
    extra = [] if into is None else [into]
    return pl.pallas_call(
        nodes_grad_kernel,
        grid=(steps,),
        in_specs=[SMEM, rows_spec(n, first), VMEM] + [ANY] * len((*extra, *behind)),
        out_specs=[rows_spec(d, first), SMEM],
        out_shape=[jax.ShapeDtypeStruct((n, d), BF16), CTL],
        input_output_aliases={3: 0} if extra else {},
        compiler_params=params(5),
        cost_estimate=cost(2 * steps * TILE * d * n, (n + 2 * steps * TILE) * d * 2),
        name="nodes_grad",
    )(ctl, table, spread, *extra, *behind)


def swap(value, bit):
    return lax.ppermute(value, AXES, [(i, i ^ bit) for i in range(32)])


def after(value, *others):
    return lax.optimization_barrier((value, *others))[0]


def codes_of(*bits):
    order = [0]
    for group in bits:
        order = [code ^ g for g in group for code in order]
    return order


def with_bias(odd, weight, bias):
    rows = bias.shape[0]
    lanes = jnp.concatenate([bias, bias])
    mine = (jnp.arange(EXTRA) >= rows) == odd
    head = jnp.where(mine, lanes, 0).astype(BF16)[None, :]
    tail = jnp.where(jnp.arange(rows)[:, None] == 0, head, 0).astype(BF16)
    return jnp.concatenate([weight, tail], axis=1)


def cat(*parts):
    return jnp.concatenate(parts, axis=0)


def fast(nodes, weight, bias, neighbours, degree, counts, cotangent):
    me = (lax.axis_index("clus") * 4 + lax.axis_index("rep")).astype(jnp.int32)[None]
    ctl = cat(me, counts)
    rows, m = weight.shape
    half = m // 2
    nb = neighbours.T
    deg = degree[None, :]
    steps = nodes.shape[0] // TILE

    odd = me % 2 == 1
    own = with_bias(odd, weight, bias)
    one, two = swap(own, Z1), swap(own, Z2)
    table, ctl = neighbour_table(after(ctl, own), nb, deg)
    one, two = after(one, ctl), after(two, ctl)
    three = swap(two, Z1)
    agg, ctl, table = aggregate(after(ctl, two), deg, table, nodes, 0, 2)
    three = after(three, ctl)
    heads = jnp.concatenate([own[:1, m:], one[:1, m:], two[:1, m:], three[:1, m:]], axis=1)
    heads = jnp.pad(heads, ((0, HEAD - 1), (0, half - 4 * EXTRA)))
    p = cat(own[:, :half], one[:, :half], two[:, :half], three[:, :half], heads)
    q = cat(own[:, half:m], one[:, half:m], two[:, half:m], three[:, half:m])
    px, qy = swap(p, X), swap(q, Y)
    agg, ctl, table = aggregate(after(ctl, p, q), deg, table, nodes, 2, 4, agg)
    px, qy = after(px, ctl), after(qy, ctl)
    p, q = cat(p, px), cat(q, qy)
    py, qx = swap(p, Y), swap(q, X)
    p_other, q_other = swap(p, CORE), swap(q, CORE)
    agg, ctl, table = aggregate(after(ctl, p, q), deg, table, nodes, 6, steps - 6, agg)
    zs = (0, Z1, Z2, Z1 ^ Z2)
    near_p, near_q = codes_of(zs, (0, X)), codes_of(zs, (0, Y))

    def ends(flip_p, flip_q):
        order_p, order_q = [c ^ flip_p for c in near_p], [c ^ flip_q for c in near_q]
        mine = (order_p, 0, True), (order_q, half, False)
        return *mine, *[([c ^ CORE for c in order], col, headed) for order, col, headed in mine]

    *full, ctl = place(ctl, (p, q, p_other, q_other), ends(0, 0), (32 * rows, m))
    part, ctl, agg = near_product(ctl, agg, full[0])
    py, qx = after(py, ctl), after(qx, ctl)
    py_other, qx_other = swap(py, CORE), swap(qx, CORE)
    far = ends(Y, X)
    *full, ctl = place(ctl, (py, qx), far[:2], (32 * rows, m), full)
    py_other, qx_other = after(py_other, ctl), after(qx_other, ctl)
    full, bias_full, ctl = place(ctl, (py_other, qx_other), far[2:], (32 * rows, m), full)
    act, grad, bias_sum, ctl, agg = forward(ctl, agg, full, bias_full, cotangent, part)

    terms, ctl, agg = wgrad(ctl, agg, grad, bias_sum, 1, 4)
    got = swap(terms, CORE)
    mine, ctl, agg = wgrad(ctl, agg, grad, bias_sum, 2, 3)
    got = after(got, ctl)

    def total(*parts):
        return functools.reduce(jnp.add, [part.astype(F32) for part in parts])

    send_p = total(mine[1:, :, :half], got[2:, :, :half]).astype(BF16)
    send_q = total(mine[::2, :TILE, half:], got[1::2, :TILE, half:]).astype(BF16)
    got_p, got_q = swap(send_p, Y), swap(send_q, X)
    kept, ctl, _ = wgrad(after(ctl, send_p, send_q), agg, grad, bias_sum, 0, 1)
    spread, ctl = agg_grad(ctl, deg, grad, full)
    got_p, got_q = after(got_p, ctl), after(got_q, ctl)
    last = 3 * rows
    next_p = total(mine[0, :, :half], got[1, :, :half], got_p[1]).astype(BF16)
    next_q = total(mine[1, :TILE, half:], got[2, :TILE, half:], got_q[1]).astype(BF16)
    sends = next_p[last:], next_q[last:], next_p[:last], next_q[:last]
    early_p, early_q, late_p, late_q = [swap(part, bit) for part, bit in zip(sends, (X, Y, X, Y))]
    out, ctl = nodes_grad(ctl, table, spread, 0, 2, behind=sends)
    early_p, early_q = after(early_p, ctl), after(early_q, ctl)

    def piece(i):
        at, head, lanes = slice(i * rows, (i + 1) * rows), slice(TILE, TILE + 1), slice(i * EXTRA, (i + 1) * EXTRA)
        more_p, more_q = (early_p[:rows], early_q) if i == 3 else (late_p[at], late_q[at])
        p = total(kept[0, at, :half], got[0, at, :half], got_p[0, at], more_p)
        q = total(kept[0, at, half:], got[0, at, half:], got_q[0, at], more_q)
        ends = total(kept[0, head, lanes], got[0, head, lanes], got_p[0, head, lanes], early_p[rows : rows + 1, lanes])
        return jnp.concatenate([p, q, jnp.pad(ends, ((0, rows - 1), (0, 0)))], axis=1)

    third = piece(3).astype(BF16)
    far = swap(third, Z1)
    out, ctl = nodes_grad(ctl, table, spread, 2, 2, out, behind=(third,))
    far, late_p, late_q = after(far, ctl), after(late_p, ctl), after(late_q, ctl)
    second, first = (piece(2) + far.astype(F32)).astype(BF16), piece(1).astype(BF16)
    mid, near = swap(second, Z2), swap(first, Z1)
    out, ctl = nodes_grad(ctl, table, spread, 4, steps - 4, out, behind=(second, first))
    near, mid = after(near, ctl), after(mid, ctl)
    own_rows = piece(0)
    weight_grad = total(own_rows[:, :m], near[:, :m], mid[:, :m])
    ends = total(own_rows[0, m:], near[0, m:], mid[0, m:])
    return act, out, weight_grad, jnp.where(odd, ends[rows:], ends[:rows])


def general(nodes, weight, bias, neighbours, degree, counts, cotangent):
    ctl = cat(jnp.zeros_like(counts), counts)
    nb = neighbours.T
    deg = degree[None, :]
    steps = nodes.shape[0] // TILE
    full = lax.all_gather(weight, AXES, axis=0, tiled=True)
    bias_full = lax.all_gather(bias, AXES, axis=0, tiled=True).astype(F32)[None, :]
    table, _ = neighbour_table(ctl, nb, deg)
    agg, _, table = aggregate(ctl, deg, table, nodes, 0, steps)
    act, grad, bias_sum, _, agg = forward(ctl, agg, full, bias_full, cotangent)
    term = lax.dot_general(agg, grad, TN, preferred_element_type=F32)
    weight_grad = lax.psum_scatter(term, AXES, scatter_dimension=0, tiled=True)
    bias_grad = lax.psum_scatter(bias_sum[0], AXES, scatter_dimension=0, tiled=True)
    spread, _ = agg_grad(ctl, deg, grad, full)
    out, _ = nodes_grad(ctl, table, spread, 0, steps)
    return act, out, weight_grad, bias_grad


def solution(mesh):
    both = P(AXES, None)
    one = P(AXES)
    cube = (mesh.shape["clus"], mesh.shape["rep"]) == (8, 4)
    return jax.shard_map(
        fast if cube else general,
        mesh=mesh,
        in_specs=(both, both, one, both, one, one, both),
        out_specs=(both, both, both, one),
        check_vma=False,
    )
```

```python
import functools

import jax
import jax.numpy as jnp
from jax import lax
from jax.experimental import pallas as pl
from jax.experimental.pallas import tpu as pltpu
from jax.sharding import PartitionSpec as P

AXES = ("clus", "rep")
MIB = 2**20
F32 = jnp.float32
BF16 = jnp.bfloat16
Z1, Z2, CORE, X, Y = 1, 2, 4, 8, 16
ANY = pl.BlockSpec(memory_space=pl.ANY)
SMEM = pl.BlockSpec(memory_space=pltpu.SMEM)
TN = (((0,), (0,)), ((), ()))
NT = (((1,), (1,)), ((), ()))
NN = (((1,), (0,)), ((), ()))
VMEM = pl.BlockSpec(memory_space=pltpu.VMEM)
HBM = pl.BlockSpec(memory_space=pltpu.HBM)
EXTRA = 128
HEAD = 16


def params(mib=12):
    return pltpu.CompilerParams(vmem_limit_bytes=int(mib * MIB))


def cost(flops, nbytes):
    return pl.CostEstimate(flops=flops, bytes_accessed=nbytes, transcendentals=0)


def column(row):
    return jnp.transpose(jnp.broadcast_to(row, (8, row.shape[1])))[:, :1]


def scale_row(start, degree, count):
    slots = start + lax.broadcasted_iota(jnp.int32, degree.shape, 1)
    live = (slots < count).astype(F32)
    return live / (degree.astype(F32) + 1.0)


def table_kernel(ctl, used, table, ctl_out):
    hand_on(ctl, ctl_out)
    quarter = table.shape[0] // 4
    fan, tile = used.shape
    chunk = min(quarter, 128)
    slots = used[...]
    word = jnp.where(slots >= 0, slots % quarter, -1)
    value = jnp.left_shift(1, jnp.maximum(slots, 0) // quarter * 8)
    own = pl.program_id(0) * tile + lax.broadcasted_iota(jnp.int32, (1, tile), 1)
    own_word, own_value = own % quarter, jnp.left_shift(2, own // quarter * 8)
    words = lax.broadcasted_iota(jnp.int32, (chunk, tile), 0)

    def build(c, carry):
        base = c * chunk
        at = words + base
        acc = jnp.where(at == own_word, own_value, 0)
        for k in range(fan):
            acc = acc + jnp.where(at == word[k : k + 1, :], value[k : k + 1, :], 0)
        for part in range(4):
            counts = jnp.bitwise_and(jnp.right_shift(acc, 8 * part), 255)
            rows = pl.ds(pl.multiple_of(part * quarter + base, chunk), chunk)
            table[rows, :] = counts.astype(F32).astype(BF16)
        return carry

    lax.fori_loop(0, quarter // chunk, build, 0)


def neighbour_table(ctl, nb, deg):
    fan, n = nb.shape
    used = jnp.where(jnp.arange(fan, dtype=jnp.int32)[:, None] < deg, nb, -1)
    return pl.pallas_call(
        table_kernel,
        grid=(n // TILE,),
        in_specs=[
            SMEM,
            pl.BlockSpec((fan, TILE), lambda t: (0, t)),
        ],
        out_specs=[pl.BlockSpec((n, TILE), lambda t: (0, t)), SMEM],
        out_shape=[pltpu.HBM((n, n), BF16), CTL],
        compiler_params=params(6),
        cost_estimate=cost(n * n * n, n * n * 2),
        name="table",
    )(ctl, used)


TILE = 256


def scaled(ctl, deg, t, value):
    at = pl.multiple_of(t * TILE, TILE)
    return (value * column(scale_row(at, deg[:, pl.ds(at, TILE)], ctl[1]))).astype(BF16)


CTL = jax.ShapeDtypeStruct((2,), jnp.int32)


def hand_on(ctl, ctl_out):
    ctl_out[0] = ctl[0]
    ctl_out[1] = ctl[1]


def rows_spec(width, first=0):
    return pl.BlockSpec((TILE, width), lambda t: (t + first, 0))


def aggregate_kernel(first, ctl, deg, table, nodes, *rest):
    out, ctl_out, _ = rest[-3:]
    hand_on(ctl, ctl_out)
    t = pl.program_id(0) + first
    value = lax.dot_general(table[...], nodes[...], TN, preferred_element_type=F32)
    out[...] = scaled(ctl, deg, t, value)


def aggregate(ctl, deg, table, nodes, first, steps, into=None):
    n, d = nodes.shape
    extra = [] if into is None else [into]
    return pl.pallas_call(
        functools.partial(aggregate_kernel, first),
        grid=(steps,),
        in_specs=[SMEM, VMEM, pl.BlockSpec((n, TILE), lambda t: (0, t + first)), VMEM] + [ANY] * len(extra),
        out_specs=[rows_spec(d, first), SMEM, ANY],
        out_shape=[pltpu.HBM((n, d), BF16), CTL, pltpu.HBM((n, n), BF16)],
        input_output_aliases={2: 2, 4: 0} if extra else {2: 2},
        compiler_params=params(6.5),
        cost_estimate=cost(2 * steps * TILE * d * n, (n + 2 * steps * TILE) * d * 2),
        name="aggregate",
    )(ctl, deg, table, nodes, *extra)


def halves(ctl, width, far):
    y, x = ctl[0] // 16, lax.rem(ctl[0] // 8, 2)
    if far:
        y, x = 1 - y, 1 - x
    two, four = width // 2, width // 4
    return [(y * two, two)], [(x * four, four), (two + x * four, four)]


def half_product(agg, weight, where, at):
    parts = []
    for start, length in where:
        rows = pl.ds(pl.multiple_of(start, length), length)
        parts.append(jnp.dot(agg[:, rows], weight[rows, at], preferred_element_type=F32))
    return functools.reduce(jnp.add, parts)


def near_kernel(ctl, agg, weight, part, ctl_out, _):
    hand_on(ctl, ctl_out)
    d, m = weight.shape
    for side, where in enumerate(halves(ctl, d, False)):
        at = slice(side * m // 2, (side + 1) * m // 2)
        part[:, at] = half_product(agg, weight, where, at).astype(BF16)


def near_product(ctl, agg, weight):
    n, d = agg.shape
    m = weight.shape[1]
    return pl.pallas_call(
        near_kernel,
        grid=(n // TILE,),
        in_specs=[SMEM, rows_spec(d), VMEM],
        out_specs=[rows_spec(m), SMEM, ANY],
        out_shape=[pltpu.HBM((n, m), BF16), CTL, pltpu.HBM((n, d), BF16)],
        input_output_aliases={1: 2},
        compiler_params=params(8),
        cost_estimate=cost(n * d * m, 8 * n * m),
        name="near",
    )(ctl, agg, weight)


def forward_kernel(split, ctl, agg, weight, bias, cot, *refs):
    act, grad, bias_sum, ctl_out, _ = refs[-5:]
    hand_on(ctl, ctl_out)
    t = pl.program_id(0)
    d, m = weight.shape
    half = m // 2

    @pl.when(t == 0)
    def _():
        bias_sum[...] = jnp.zeros_like(bias_sum)

    slots = t * TILE + lax.broadcasted_iota(jnp.int32, (TILE, EXTRA), 0)
    live = (slots < ctl[1]).astype(F32).astype(BF16)
    live = jnp.concatenate([live] * (half // EXTRA), axis=1)
    for side, where in enumerate(halves(ctl, d, True)):
        at = slice(side * half, (side + 1) * half)
        if split:
            pre = half_product(agg, weight, where, at) + refs[0][:, at].astype(F32) + bias[:, at]
        else:
            pre = jnp.dot(agg[...], weight[:, at], preferred_element_type=F32) + bias[:, at]
        sig = jax.nn.sigmoid(pre)
        silu = pre * sig
        act[:, at] = silu.astype(BF16) * live
        slope = (cot[:, at] * live).astype(F32) * (sig + silu * (1.0 - sig))
        grad[:, at] = slope.astype(BF16)
        bias_sum[:, at] += jnp.sum(slope, axis=0, keepdims=True)


def forward(ctl, agg, weight, bias, cot, *part):
    n, d = agg.shape
    m = weight.shape[1]
    return pl.pallas_call(
        functools.partial(forward_kernel, bool(part)),
        grid=(n // TILE,),
        in_specs=[SMEM, rows_spec(d), VMEM, VMEM, rows_spec(m)] + [rows_spec(m)] * len(part),
        out_specs=[rows_spec(m), rows_spec(m), VMEM, SMEM, ANY],
        out_shape=[
            pltpu.HBM((n, m), BF16),
            jax.ShapeDtypeStruct((n, m), BF16),
            jax.ShapeDtypeStruct((1, m), F32),
            CTL,
            pltpu.HBM((n, d), BF16),
        ],
        input_output_aliases={1: 4, 5: 0} if part else {1: 4},
        compiler_params=params(14),
        cost_estimate=cost(2 * n * d * m, 5 * n * m * 2),
        name="forward",
    )(ctl, agg, weight, bias, cot, *part)


def place_kernel(codes, ctl, *refs):
    pieces, refs = refs[: len(codes)], refs[len(codes) :]
    weight, bias, ctl_out, heads, weight_sem, head_sem = refs[-6:]
    hand_on(ctl, ctl_out)
    half = weight.shape[1] // 2
    rows = weight.shape[0] // 32
    copies, head_copies, pairs = [], [], []
    for (order, col, headed), piece in zip(codes, pieces):
        group = 4 * rows + HEAD * headed
        for i, code in enumerate(order):
            owner = lax.bitwise_xor(ctl[0], code)
            start = i // 4 * group + i % 4 * rows
            copies.append(
                pltpu.make_async_copy(
                    piece.at[pl.ds(start, rows), :],
                    weight.at[pl.ds(pl.multiple_of(owner * rows, rows), rows), pl.ds(col, half)],
                    weight_sem.at[len(copies)],
                )
            )
            if headed and i % 4 == 0:
                k = len(head_copies)
                head = piece.at[pl.ds(start + 4 * rows, HEAD), pl.ds(0, 4 * EXTRA)]
                head_copies.append(pltpu.make_async_copy(head, heads.at[k], head_sem.at[k]))
            if headed and i % 2 == 0:
                pairs.append((i % 4 * EXTRA, len(head_copies) - 1, owner // 2))
    for c in copies + head_copies:
        c.start()
    bias[...] = refs[1][...] if len(refs) == 8 else jnp.zeros_like(bias)
    for c in head_copies:
        c.wait()
    for lane, k, pair in pairs:
        one = heads[k, :1, lane : lane + EXTRA].astype(F32)
        two = heads[k, :1, lane + EXTRA : lane + 2 * EXTRA].astype(F32)
        bias[:, pl.ds(pl.multiple_of(pair * EXTRA, EXTRA), EXTRA)] = one + two
    for c in copies:
        c.wait()


def place(ctl, pieces, codes, shape, into=()):
    total = sum(len(order) for order, _, _ in codes)
    first = 1 + len(pieces)
    return pl.pallas_call(
        functools.partial(place_kernel, codes),
        in_specs=[SMEM] + [ANY] * len(pieces) + ([ANY, VMEM] if into else []),
        out_specs=[ANY, VMEM, SMEM],
        out_shape=[jax.ShapeDtypeStruct(shape, BF16), jax.ShapeDtypeStruct((1, shape[1]), F32), CTL],
        input_output_aliases={first: 0} if into else {},
        scratch_shapes=[
            pltpu.VMEM((total // 8, HEAD, 4 * EXTRA), BF16),
            pltpu.SemaphoreType.DMA((total,)),
            pltpu.SemaphoreType.DMA((total // 8,)),
        ],
        compiler_params=params(2),
        cost_estimate=cost(0, 2 * shape[0] * shape[1]),
        name="place",
    )(ctl, *pieces, *into)


def terms_of(me, tile, value, bias_sum, out):
    count, m = value.shape
    rows = count // 4
    z = lax.rem(me, 4)
    out[count:, :] = jnp.zeros((HEAD, m), BF16)
    top = lax.broadcasted_iota(jnp.int32, (HEAD, EXTRA), 0) == 0
    for q in range(4):
        place = lax.bitwise_xor(z, q)
        out[pl.ds(pl.multiple_of(place * rows, rows), rows), :] = value[q * rows : (q + 1) * rows, :].astype(BF16)
        pair = bias_sum[:, pl.ds(pl.multiple_of(tile * TILE + q // 2 * EXTRA, EXTRA), EXTRA)]
        out[count:, pl.ds(pl.multiple_of(place * EXTRA, EXTRA), EXTRA)] = jnp.where(top, pair, 0.0).astype(BF16)


def wgrad_kernel(code, ctl, agg, grad, bias_sum, out, ctl_out, _):
    hand_on(ctl, ctl_out)
    tile = lax.bitwise_xor(ctl[0] // 4, 2 * pl.program_id(0) + code)
    value = lax.dot_general(agg[...], grad[...], TN, preferred_element_type=F32)
    terms_of(ctl[0], tile, value, bias_sum, out.at[0])


def wgrad(ctl, agg, grad, bias_sum, code, steps):
    n, d = agg.shape
    m = grad.shape[1]
    return pl.pallas_call(
        functools.partial(wgrad_kernel, code),
        grid_spec=pltpu.PrefetchScalarGridSpec(
            num_scalar_prefetch=1,
            grid=(steps,),
            in_specs=[
                pl.BlockSpec((n, TILE), lambda t, ctl: (0, (ctl[0] // 4) ^ (2 * t + code))),
                VMEM,
                VMEM,
            ],
            out_specs=[pl.BlockSpec((1, TILE + HEAD, m), lambda t, ctl: (t, 0, 0)), SMEM, ANY],
        ),
        out_shape=[jax.ShapeDtypeStruct((steps, TILE + HEAD, m), BF16), CTL, pltpu.HBM((n, d), BF16)],
        input_output_aliases={1: 2},
        compiler_params=params(8),
        cost_estimate=cost(2 * n * TILE * steps * m, 2 * n * m * 2),
        name="wgrad",
    )(ctl, agg, grad, bias_sum)


def agg_grad_kernel(ctl, deg, grad, weight, out, ctl_out):
    hand_on(ctl, ctl_out)
    value = lax.dot_general(grad[...], weight[...], NT, preferred_element_type=F32)
    out[...] = scaled(ctl, deg, pl.program_id(0), value)


def agg_grad(ctl, deg, grad, weight):
    n, m = grad.shape
    d = weight.shape[0]
    return pl.pallas_call(
        agg_grad_kernel,
        grid=(n // TILE,),
        in_specs=[SMEM, VMEM, rows_spec(m), VMEM],
        out_specs=[rows_spec(d), SMEM],
        out_shape=[jax.ShapeDtypeStruct((n, d), BF16), CTL],
        compiler_params=params(5),
        cost_estimate=cost(2 * n * d * m, 3 * n * m * 2),
        name="agg_grad",
    )(ctl, deg, grad, weight)


def nodes_grad_kernel(ctl, table, spread, *rest):
    out, ctl_out = rest[-2:]
    hand_on(ctl, ctl_out)
    out[...] = jnp.dot(table[...], spread[...], preferred_element_type=F32).astype(BF16)


def nodes_grad(ctl, table, spread, first, steps, into=None, behind=()):
    n, d = spread.shape
    extra = [] if into is None else [into]
    return pl.pallas_call(
        nodes_grad_kernel,
        grid=(steps,),
        in_specs=[SMEM, rows_spec(n, first), VMEM] + [ANY] * len((*extra, *behind)),
        out_specs=[rows_spec(d, first), SMEM],
        out_shape=[jax.ShapeDtypeStruct((n, d), BF16), CTL],
        input_output_aliases={3: 0} if extra else {},
        compiler_params=params(5),
        cost_estimate=cost(2 * steps * TILE * d * n, (n + 2 * steps * TILE) * d * 2),
        name="nodes_grad",
    )(ctl, table, spread, *extra, *behind)


def swap(value, bit):
    return lax.ppermute(value, AXES, [(i, i ^ bit) for i in range(32)])


def after(value, *others):
    return lax.optimization_barrier((value, *others))[0]


def codes_of(*bits):
    order = [0]
    for group in bits:
        order = [code ^ g for g in group for code in order]
    return order


def with_bias(odd, weight, bias):
    rows = bias.shape[0]
    lanes = jnp.concatenate([bias, bias])
    mine = (jnp.arange(EXTRA) >= rows) == odd
    head = jnp.where(mine, lanes, 0).astype(BF16)[None, :]
    tail = jnp.where(jnp.arange(rows)[:, None] == 0, head, 0).astype(BF16)
    return jnp.concatenate([weight, tail], axis=1)


def cat(*parts):
    return jnp.concatenate(parts, axis=0)


def fast(nodes, weight, bias, neighbours, degree, counts, cotangent):
    me = (lax.axis_index("clus") * 4 + lax.axis_index("rep")).astype(jnp.int32)[None]
    ctl = cat(me, counts)
    rows, m = weight.shape
    half = m // 2
    nb = neighbours.T
    deg = degree[None, :]
    steps = nodes.shape[0] // TILE

    odd = me % 2 == 1
    own = with_bias(odd, weight, bias)
    one, two = swap(own, Z1), swap(own, Z2)
    table, ctl = neighbour_table(after(ctl, own), nb, deg)
    one, two = after(one, ctl), after(two, ctl)
    three = swap(two, Z1)
    agg, ctl, table = aggregate(after(ctl, two), deg, table, nodes, 0, 2)
    three = after(three, ctl)
    heads = jnp.concatenate([own[:1, m:], one[:1, m:], two[:1, m:], three[:1, m:]], axis=1)
    heads = jnp.pad(heads, ((0, HEAD - 1), (0, half - 4 * EXTRA)))
    p = cat(own[:, :half], one[:, :half], two[:, :half], three[:, :half], heads)
    q = cat(own[:, half:m], one[:, half:m], two[:, half:m], three[:, half:m])
    px, qy = swap(p, X), swap(q, Y)
    agg, ctl, table = aggregate(after(ctl, p, q), deg, table, nodes, 2, 4, agg)
    px, qy = after(px, ctl), after(qy, ctl)
    p, q = cat(p, px), cat(q, qy)
    py, qx = swap(p, Y), swap(q, X)
    p_other, q_other = swap(p, CORE), swap(q, CORE)
    agg, ctl, table = aggregate(after(ctl, p, q), deg, table, nodes, 6, steps - 6, agg)
    zs = (0, Z1, Z2, Z1 ^ Z2)
    near_p, near_q = codes_of(zs, (0, X)), codes_of(zs, (0, Y))

    def ends(flip_p, flip_q):
        order_p, order_q = [c ^ flip_p for c in near_p], [c ^ flip_q for c in near_q]
        mine = (order_p, 0, True), (order_q, half, False)
        return *mine, *[([c ^ CORE for c in order], col, headed) for order, col, headed in mine]

    *full, ctl = place(ctl, (p, q, p_other, q_other), ends(0, 0), (32 * rows, m))
    part, ctl, agg = near_product(ctl, agg, full[0])
    py, qx = after(py, ctl), after(qx, ctl)
    py_other, qx_other = swap(py, CORE), swap(qx, CORE)
    far = ends(Y, X)
    *full, ctl = place(ctl, (py, qx), far[:2], (32 * rows, m), full)
    py_other, qx_other = after(py_other, ctl), after(qx_other, ctl)
    full, bias_full, ctl = place(ctl, (py_other, qx_other), far[2:], (32 * rows, m), full)
    act, grad, bias_sum, ctl, agg = forward(ctl, agg, full, bias_full, cotangent, part)

    terms, ctl, agg = wgrad(ctl, agg, grad, bias_sum, 1, 4)
    got = swap(terms, CORE)
    mine, ctl, agg = wgrad(ctl, agg, grad, bias_sum, 2, 3)
    got = after(got, ctl)

    def total(*parts):
        return functools.reduce(jnp.add, [part.astype(F32) for part in parts])

    send_p = total(mine[1:, :, :half], got[2:, :, :half]).astype(BF16)
    send_q = total(mine[::2, :TILE, half:], got[1::2, :TILE, half:]).astype(BF16)
    got_p, got_q = swap(send_p, Y), swap(send_q, X)
    kept, ctl, _ = wgrad(after(ctl, send_p, send_q), agg, grad, bias_sum, 0, 1)
    spread, ctl = agg_grad(ctl, deg, grad, full)
    got_p, got_q = after(got_p, ctl), after(got_q, ctl)
    last = 3 * rows
    next_p = total(mine[0, :, :half], got[1, :, :half], got_p[1]).astype(BF16)
    next_q = total(mine[1, :TILE, half:], got[2, :TILE, half:], got_q[1]).astype(BF16)
    sends = next_p[last:], next_q[last:], next_p[:last], next_q[:last]
    early_p, early_q, late_p, late_q = [swap(part, bit) for part, bit in zip(sends, (X, Y, X, Y))]
    out, ctl = nodes_grad(ctl, table, spread, 0, 2, behind=sends)
    early_p, early_q = after(early_p, ctl), after(early_q, ctl)

    def piece(i):
        at, head, lanes = slice(i * rows, (i + 1) * rows), slice(TILE, TILE + 1), slice(i * EXTRA, (i + 1) * EXTRA)
        more_p, more_q = (early_p[:rows], early_q) if i == 3 else (late_p[at], late_q[at])
        p = total(kept[0, at, :half], got[0, at, :half], got_p[0, at], more_p)
        q = total(kept[0, at, half:], got[0, at, half:], got_q[0, at], more_q)
        ends = total(kept[0, head, lanes], got[0, head, lanes], got_p[0, head, lanes], early_p[rows : rows + 1, lanes])
        return jnp.concatenate([p, q, jnp.pad(ends, ((0, rows - 1), (0, 0)))], axis=1)

    third = piece(3).astype(BF16)
    far = swap(third, Z1)
    out, ctl = nodes_grad(ctl, table, spread, 2, 2, out, behind=(third,))
    far, late_p, late_q = after(far, ctl), after(late_p, ctl), after(late_q, ctl)
    second, first = (piece(2) + far.astype(F32)).astype(BF16), piece(1).astype(BF16)
    mid, near = swap(second, Z2), swap(first, Z1)
    out, ctl = nodes_grad(ctl, table, spread, 4, steps - 4, out, behind=(second, first))
    near, mid = after(near, ctl), after(mid, ctl)
    own_rows = piece(0)
    weight_grad = total(own_rows[:, :m], near[:, :m], mid[:, :m])
    ends = total(own_rows[0, m:], near[0, m:], mid[0, m:])
    return act, out, weight_grad, jnp.where(odd, ends[rows:], ends[:rows])


def general(nodes, weight, bias, neighbours, degree, counts, cotangent):
    ctl = cat(jnp.zeros_like(counts), counts)
    nb = neighbours.T
    deg = degree[None, :]
    steps = nodes.shape[0] // TILE
    full = lax.all_gather(weight, AXES, axis=0, tiled=True)
    bias_full = lax.all_gather(bias, AXES, axis=0, tiled=True).astype(F32)[None, :]
    table, _ = neighbour_table(ctl, nb, deg)
    agg, _, table = aggregate(ctl, deg, table, nodes, 0, steps)
    act, grad, bias_sum, _, agg = forward(ctl, agg, full, bias_full, cotangent)
    term = lax.dot_general(agg, grad, TN, preferred_element_type=F32)
    weight_grad = lax.psum_scatter(term, AXES, scatter_dimension=0, tiled=True)
    bias_grad = lax.psum_scatter(bias_sum[0], AXES, scatter_dimension=0, tiled=True)
    spread, _ = agg_grad(ctl, deg, grad, full)
    out, _ = nodes_grad(ctl, table, spread, 0, steps)
    return act, out, weight_grad, bias_grad


def solution(mesh):
    both = P(AXES, None)
    one = P(AXES)
    cube = (mesh.shape["clus"], mesh.shape["rep"]) == (8, 4)
    return jax.shard_map(
        fast if cube else general,
        mesh=mesh,
        in_specs=(both, both, one, both, one, one, both),
        out_specs=(both, both, both, one),
        check_vma=False,
    )
```

```python
import functools

import jax
import jax.numpy as jnp
from jax import lax
from jax.experimental import pallas as pl
from jax.experimental.pallas import tpu as pltpu
from jax.sharding import PartitionSpec as P

AXES = ("clus", "rep")
MIB = 2**20
F32 = jnp.float32
BF16 = jnp.bfloat16
Z1, Z2, CORE, X, Y = 1, 2, 4, 8, 16
ANY = pl.BlockSpec(memory_space=pl.ANY)
SMEM = pl.BlockSpec(memory_space=pltpu.SMEM)
TN = (((0,), (0,)), ((), ()))
NT = (((1,), (1,)), ((), ()))
NN = (((1,), (0,)), ((), ()))
VMEM = pl.BlockSpec(memory_space=pltpu.VMEM)
HBM = pl.BlockSpec(memory_space=pltpu.HBM)
EXTRA = 128
HEAD = 16


def params(mib=12):
    return pltpu.CompilerParams(vmem_limit_bytes=int(mib * MIB))


def cost(flops, nbytes):
    return pl.CostEstimate(flops=flops, bytes_accessed=nbytes, transcendentals=0)


def column(row):
    return jnp.transpose(jnp.broadcast_to(row, (8, row.shape[1])))[:, :1]


def scale_row(start, degree, count):
    slots = start + lax.broadcasted_iota(jnp.int32, degree.shape, 1)
    live = (slots < count).astype(F32)
    return live / (degree.astype(F32) + 1.0)


def table_kernel(ctl, used, table, ctl_out):
    hand_on(ctl, ctl_out)
    quarter = table.shape[0] // 4
    fan, tile = used.shape
    chunk = min(quarter, 128)
    slots = used[...]
    word = jnp.where(slots >= 0, slots % quarter, -1)
    value = jnp.left_shift(1, jnp.maximum(slots, 0) // quarter * 8)
    own = pl.program_id(0) * tile + lax.broadcasted_iota(jnp.int32, (1, tile), 1)
    own_word, own_value = own % quarter, jnp.left_shift(2, own // quarter * 8)
    words = lax.broadcasted_iota(jnp.int32, (chunk, tile), 0)

    def build(c, carry):
        base = c * chunk
        at = words + base
        acc = jnp.where(at == own_word, own_value, 0)
        for k in range(fan):
            acc = acc + jnp.where(at == word[k : k + 1, :], value[k : k + 1, :], 0)
        for part in range(4):
            counts = jnp.bitwise_and(jnp.right_shift(acc, 8 * part), 255)
            rows = pl.ds(pl.multiple_of(part * quarter + base, chunk), chunk)
            table[rows, :] = counts.astype(F32).astype(BF16)
        return carry

    lax.fori_loop(0, quarter // chunk, build, 0)


def neighbour_table(ctl, nb, deg):
    fan, n = nb.shape
    used = jnp.where(jnp.arange(fan, dtype=jnp.int32)[:, None] < deg, nb, -1)
    return pl.pallas_call(
        table_kernel,
        grid=(n // TILE,),
        in_specs=[
            SMEM,
            pl.BlockSpec((fan, TILE), lambda t: (0, t)),
        ],
        out_specs=[pl.BlockSpec((n, TILE), lambda t: (0, t)), SMEM],
        out_shape=[pltpu.HBM((n, n), BF16), CTL],
        compiler_params=params(6),
        cost_estimate=cost(n * n * n, n * n * 2),
        name="table",
    )(ctl, used)


TILE = 256


def scaled(ctl, deg, t, value):
    at = pl.multiple_of(t * TILE, TILE)
    return (value * column(scale_row(at, deg[:, pl.ds(at, TILE)], ctl[1]))).astype(BF16)


CTL = jax.ShapeDtypeStruct((2,), jnp.int32)


def hand_on(ctl, ctl_out):
    ctl_out[0] = ctl[0]
    ctl_out[1] = ctl[1]


def rows_spec(width, first=0):
    return pl.BlockSpec((TILE, width), lambda t: (t + first, 0))


def aggregate_kernel(first, ctl, deg, table, nodes, *rest):
    out, ctl_out, _ = rest[-3:]
    hand_on(ctl, ctl_out)
    t = pl.program_id(0) + first
    value = lax.dot_general(table[...], nodes[...], TN, preferred_element_type=F32)
    out[...] = scaled(ctl, deg, t, value)


def aggregate(ctl, deg, table, nodes, first, steps, into=None):
    n, d = nodes.shape
    extra = [] if into is None else [into]
    return pl.pallas_call(
        functools.partial(aggregate_kernel, first),
        grid=(steps,),
        in_specs=[SMEM, VMEM, pl.BlockSpec((n, TILE), lambda t: (0, t + first)), VMEM] + [ANY] * len(extra),
        out_specs=[rows_spec(d, first), SMEM, ANY],
        out_shape=[pltpu.HBM((n, d), BF16), CTL, pltpu.HBM((n, n), BF16)],
        input_output_aliases={2: 2, 4: 0} if extra else {2: 2},
        compiler_params=params(6.5),
        cost_estimate=cost(2 * steps * TILE * d * n, (n + 2 * steps * TILE) * d * 2),
        name="aggregate",
    )(ctl, deg, table, nodes, *extra)


def halves(ctl, width, far):
    y, x = ctl[0] // 16, lax.rem(ctl[0] // 8, 2)
    if far:
        y, x = 1 - y, 1 - x
    two, four = width // 2, width // 4
    return [(y * two, two)], [(x * four, four), (two + x * four, four)]


def half_product(agg, weight, where, at):
    parts = []
    for start, length in where:
        rows = pl.ds(pl.multiple_of(start, length), length)
        parts.append(jnp.dot(agg[:, rows], weight[rows, at], preferred_element_type=F32))
    return functools.reduce(jnp.add, parts)


def near_kernel(ctl, agg, weight, part, ctl_out, _):
    hand_on(ctl, ctl_out)
    d, m = weight.shape
    for side, where in enumerate(halves(ctl, d, False)):
        at = slice(side * m // 2, (side + 1) * m // 2)
        part[:, at] = half_product(agg, weight, where, at).astype(BF16)


def near_product(ctl, agg, weight):
    n, d = agg.shape
    m = weight.shape[1]
    return pl.pallas_call(
        near_kernel,
        grid=(n // TILE,),
        in_specs=[SMEM, rows_spec(d), VMEM],
        out_specs=[rows_spec(m), SMEM, ANY],
        out_shape=[pltpu.HBM((n, m), BF16), CTL, pltpu.HBM((n, d), BF16)],
        input_output_aliases={1: 2},
        compiler_params=params(8),
        cost_estimate=cost(n * d * m, 8 * n * m),
        name="near",
    )(ctl, agg, weight)


def forward_kernel(split, ctl, agg, weight, bias, cot, *refs):
    act, grad, bias_sum, ctl_out, _ = refs[-5:]
    hand_on(ctl, ctl_out)
    t = pl.program_id(0)
    d, m = weight.shape
    half = m // 2

    @pl.when(t == 0)
    def _():
        bias_sum[...] = jnp.zeros_like(bias_sum)

    slots = t * TILE + lax.broadcasted_iota(jnp.int32, (TILE, EXTRA), 0)
    live = (slots < ctl[1]).astype(F32).astype(BF16)
    live = jnp.concatenate([live] * (half // EXTRA), axis=1)
    for side, where in enumerate(halves(ctl, d, True)):
        at = slice(side * half, (side + 1) * half)
        if split:
            pre = half_product(agg, weight, where, at) + refs[0][:, at].astype(F32) + bias[:, at]
        else:
            pre = jnp.dot(agg[...], weight[:, at], preferred_element_type=F32) + bias[:, at]
        sig = jax.nn.sigmoid(pre)
        silu = pre * sig
        act[:, at] = silu.astype(BF16) * live
        slope = (cot[:, at] * live).astype(F32) * (sig + silu * (1.0 - sig))
        grad[:, at] = slope.astype(BF16)
        bias_sum[:, at] += jnp.sum(slope, axis=0, keepdims=True)


def forward(ctl, agg, weight, bias, cot, *part):
    n, d = agg.shape
    m = weight.shape[1]
    return pl.pallas_call(
        functools.partial(forward_kernel, bool(part)),
        grid=(n // TILE,),
        in_specs=[SMEM, rows_spec(d), VMEM, VMEM, rows_spec(m)] + [rows_spec(m)] * len(part),
        out_specs=[rows_spec(m), rows_spec(m), VMEM, SMEM, ANY],
        out_shape=[
            pltpu.HBM((n, m), BF16),
            jax.ShapeDtypeStruct((n, m), BF16),
            jax.ShapeDtypeStruct((1, m), F32),
            CTL,
            pltpu.HBM((n, d), BF16),
        ],
        input_output_aliases={1: 4, 5: 0} if part else {1: 4},
        compiler_params=params(14),
        cost_estimate=cost(2 * n * d * m, 5 * n * m * 2),
        name="forward",
    )(ctl, agg, weight, bias, cot, *part)


def place_kernel(codes, ctl, *refs):
    pieces, refs = refs[: len(codes)], refs[len(codes) :]
    weight, bias, ctl_out, heads, weight_sem, head_sem = refs[-6:]
    hand_on(ctl, ctl_out)
    half = weight.shape[1] // 2
    rows = weight.shape[0] // 32
    copies, head_copies, pairs = [], [], []
    for (order, col, headed), piece in zip(codes, pieces):
        group = 4 * rows + HEAD * headed
        for i, code in enumerate(order):
            owner = lax.bitwise_xor(ctl[0], code)
            start = i // 4 * group + i % 4 * rows
            copies.append(
                pltpu.make_async_copy(
                    piece.at[pl.ds(start, rows), :],
                    weight.at[pl.ds(pl.multiple_of(owner * rows, rows), rows), pl.ds(col, half)],
                    weight_sem.at[len(copies)],
                )
            )
            if headed and i % 4 == 0:
                k = len(head_copies)
                head = piece.at[pl.ds(start + 4 * rows, HEAD), pl.ds(0, 4 * EXTRA)]
                head_copies.append(pltpu.make_async_copy(head, heads.at[k], head_sem.at[k]))
            if headed and i % 2 == 0:
                pairs.append((i % 4 * EXTRA, len(head_copies) - 1, owner // 2))
    for c in copies + head_copies:
        c.start()
    bias[...] = refs[1][...] if len(refs) == 8 else jnp.zeros_like(bias)
    for c in head_copies:
        c.wait()
    for lane, k, pair in pairs:
        one = heads[k, :1, lane : lane + EXTRA].astype(F32)
        two = heads[k, :1, lane + EXTRA : lane + 2 * EXTRA].astype(F32)
        bias[:, pl.ds(pl.multiple_of(pair * EXTRA, EXTRA), EXTRA)] = one + two
    for c in copies:
        c.wait()


def place(ctl, pieces, codes, shape, into=()):
    total = sum(len(order) for order, _, _ in codes)
    first = 1 + len(pieces)
    return pl.pallas_call(
        functools.partial(place_kernel, codes),
        in_specs=[SMEM] + [ANY] * len(pieces) + ([ANY, VMEM] if into else []),
        out_specs=[ANY, VMEM, SMEM],
        out_shape=[jax.ShapeDtypeStruct(shape, BF16), jax.ShapeDtypeStruct((1, shape[1]), F32), CTL],
        input_output_aliases={first: 0} if into else {},
        scratch_shapes=[
            pltpu.VMEM((total // 8, HEAD, 4 * EXTRA), BF16),
            pltpu.SemaphoreType.DMA((total,)),
            pltpu.SemaphoreType.DMA((total // 8,)),
        ],
        compiler_params=params(2),
        cost_estimate=cost(0, 2 * shape[0] * shape[1]),
        name="place",
    )(ctl, *pieces, *into)


def terms_of(me, tile, value, bias_sum, out):
    count, m = value.shape
    rows = count // 4
    z = lax.rem(me, 4)
    out[count:, :] = jnp.zeros((HEAD, m), BF16)
    top = lax.broadcasted_iota(jnp.int32, (HEAD, EXTRA), 0) == 0
    for q in range(4):
        place = lax.bitwise_xor(z, q)
        out[pl.ds(pl.multiple_of(place * rows, rows), rows), :] = value[q * rows : (q + 1) * rows, :].astype(BF16)
        pair = bias_sum[:, pl.ds(pl.multiple_of(tile * TILE + q // 2 * EXTRA, EXTRA), EXTRA)]
        out[count:, pl.ds(pl.multiple_of(place * EXTRA, EXTRA), EXTRA)] = jnp.where(top, pair, 0.0).astype(BF16)


def wgrad_kernel(code, ctl, agg, grad, bias_sum, out, ctl_out, _):
    hand_on(ctl, ctl_out)
    tile = lax.bitwise_xor(ctl[0] // 4, 2 * pl.program_id(0) + code)
    value = lax.dot_general(agg[...], grad[...], TN, preferred_element_type=F32)
    terms_of(ctl[0], tile, value, bias_sum, out.at[0])


def wgrad(ctl, agg, grad, bias_sum, code, steps):
    n, d = agg.shape
    m = grad.shape[1]
    return pl.pallas_call(
        functools.partial(wgrad_kernel, code),
        grid_spec=pltpu.PrefetchScalarGridSpec(
            num_scalar_prefetch=1,
            grid=(steps,),
            in_specs=[
                pl.BlockSpec((n, TILE), lambda t, ctl: (0, (ctl[0] // 4) ^ (2 * t + code))),
                VMEM,
                VMEM,
            ],
            out_specs=[pl.BlockSpec((1, TILE + HEAD, m), lambda t, ctl: (t, 0, 0)), SMEM, ANY],
        ),
        out_shape=[jax.ShapeDtypeStruct((steps, TILE + HEAD, m), BF16), CTL, pltpu.HBM((n, d), BF16)],
        input_output_aliases={1: 2},
        compiler_params=params(8),
        cost_estimate=cost(2 * n * TILE * steps * m, 2 * n * m * 2),
        name="wgrad",
    )(ctl, agg, grad, bias_sum)


def agg_grad_kernel(ctl, deg, grad, weight, out, ctl_out):
    hand_on(ctl, ctl_out)
    value = lax.dot_general(grad[...], weight[...], NT, preferred_element_type=F32)
    out[...] = scaled(ctl, deg, pl.program_id(0), value)


def agg_grad(ctl, deg, grad, weight):
    n, m = grad.shape
    d = weight.shape[0]
    return pl.pallas_call(
        agg_grad_kernel,
        grid=(n // TILE,),
        in_specs=[SMEM, VMEM, rows_spec(m), VMEM],
        out_specs=[rows_spec(d), SMEM],
        out_shape=[jax.ShapeDtypeStruct((n, d), BF16), CTL],
        compiler_params=params(5),
        cost_estimate=cost(2 * n * d * m, 3 * n * m * 2),
        name="agg_grad",
    )(ctl, deg, grad, weight)


def nodes_grad_kernel(ctl, table, spread, *rest):
    out, ctl_out = rest[-2:]
    hand_on(ctl, ctl_out)
    out[...] = jnp.dot(table[...], spread[...], preferred_element_type=F32).astype(BF16)


def nodes_grad(ctl, table, spread, first, steps, into=None, behind=()):
    n, d = spread.shape
    extra = [] if into is None else [into]
    return pl.pallas_call(
        nodes_grad_kernel,
        grid=(steps,),
        in_specs=[SMEM, rows_spec(n, first), VMEM] + [ANY] * len((*extra, *behind)),
        out_specs=[rows_spec(d, first), SMEM],
        out_shape=[jax.ShapeDtypeStruct((n, d), BF16), CTL],
        input_output_aliases={3: 0} if extra else {},
        compiler_params=params(5),
        cost_estimate=cost(2 * steps * TILE * d * n, (n + 2 * steps * TILE) * d * 2),
        name="nodes_grad",
    )(ctl, table, spread, *extra, *behind)


def swap(value, bit):
    return lax.ppermute(value, AXES, [(i, i ^ bit) for i in range(32)])


def after(value, *others):
    return lax.optimization_barrier((value, *others))[0]


def codes_of(*bits):
    order = [0]
    for group in bits:
        order = [code ^ g for g in group for code in order]
    return order


def with_bias(odd, weight, bias):
    rows = bias.shape[0]
    lanes = jnp.concatenate([bias, bias])
    mine = (jnp.arange(EXTRA) >= rows) == odd
    head = jnp.where(mine, lanes, 0).astype(BF16)[None, :]
    tail = jnp.where(jnp.arange(rows)[:, None] == 0, head, 0).astype(BF16)
    return jnp.concatenate([weight, tail], axis=1)


def cat(*parts):
    return jnp.concatenate(parts, axis=0)


def fast(nodes, weight, bias, neighbours, degree, counts, cotangent):
    me = (lax.axis_index("clus") * 4 + lax.axis_index("rep")).astype(jnp.int32)[None]
    ctl = cat(me, counts)
    rows, m = weight.shape
    half = m // 2
    nb = neighbours.T
    deg = degree[None, :]
    steps = nodes.shape[0] // TILE

    odd = me % 2 == 1
    own = with_bias(odd, weight, bias)
    one, two = swap(own, Z1), swap(own, Z2)
    table, ctl = neighbour_table(after(ctl, own), nb, deg)
    one, two = after(one, ctl), after(two, ctl)
    three = swap(two, Z1)
    agg, ctl, table = aggregate(after(ctl, two), deg, table, nodes, 0, 2)
    three = after(three, ctl)
    heads = jnp.concatenate([own[:1, m:], one[:1, m:], two[:1, m:], three[:1, m:]], axis=1)
    heads = jnp.pad(heads, ((0, HEAD - 1), (0, half - 4 * EXTRA)))
    p = cat(own[:, :half], one[:, :half], two[:, :half], three[:, :half], heads)
    q = cat(own[:, half:m], one[:, half:m], two[:, half:m], three[:, half:m])
    px, qy = swap(p, X), swap(q, Y)
    agg, ctl, table = aggregate(after(ctl, p, q), deg, table, nodes, 2, 3, agg)
    px, qy = after(px, ctl), after(qy, ctl)
    p, q = cat(p, px), cat(q, qy)
    py, qx = swap(p, Y), swap(q, X)
    p_other, q_other = swap(p, CORE), swap(q, CORE)
    agg, ctl, table = aggregate(after(ctl, p, q), deg, table, nodes, 5, steps - 5, agg)
    zs = (0, Z1, Z2, Z1 ^ Z2)
    near_p, near_q = codes_of(zs, (0, X)), codes_of(zs, (0, Y))

    def ends(flip_p, flip_q):
        order_p, order_q = [c ^ flip_p for c in near_p], [c ^ flip_q for c in near_q]
        mine = (order_p, 0, True), (order_q, half, False)
        return *mine, *[([c ^ CORE for c in order], col, headed) for order, col, headed in mine]

    *full, ctl = place(ctl, (p, q, p_other, q_other), ends(0, 0), (32 * rows, m))
    part, ctl, agg = near_product(ctl, agg, full[0])
    py, qx = after(py, ctl), after(qx, ctl)
    py_other, qx_other = swap(py, CORE), swap(qx, CORE)
    far = ends(Y, X)
    *full, ctl = place(ctl, (py, qx), far[:2], (32 * rows, m), full)
    py_other, qx_other = after(py_other, ctl), after(qx_other, ctl)
    full, bias_full, ctl = place(ctl, (py_other, qx_other), far[2:], (32 * rows, m), full)
    act, grad, bias_sum, ctl, agg = forward(ctl, agg, full, bias_full, cotangent, part)

    terms, ctl, agg = wgrad(ctl, agg, grad, bias_sum, 1, 4)
    got = swap(terms, CORE)
    mine, ctl, agg = wgrad(ctl, agg, grad, bias_sum, 2, 3)
    got = after(got, ctl)

    def total(*parts):
        return functools.reduce(jnp.add, [part.astype(F32) for part in parts])

    send_p = total(mine[1:, :, :half], got[2:, :, :half]).astype(BF16)
    send_q = total(mine[::2, :TILE, half:], got[1::2, :TILE, half:]).astype(BF16)
    got_p, got_q = swap(send_p, Y), swap(send_q, X)
    kept, ctl, _ = wgrad(after(ctl, send_p, send_q), agg, grad, bias_sum, 0, 1)
    spread, ctl = agg_grad(ctl, deg, grad, full)
    got_p, got_q = after(got_p, ctl), after(got_q, ctl)
    last = 3 * rows
    next_p = total(mine[0, :, :half], got[1, :, :half], got_p[1]).astype(BF16)
    next_q = total(mine[1, :TILE, half:], got[2, :TILE, half:], got_q[1]).astype(BF16)
    sends = next_p[last:], next_q[last:], next_p[:last], next_q[:last]
    early_p, early_q, late_p, late_q = [swap(part, bit) for part, bit in zip(sends, (X, Y, X, Y))]
    out, ctl = nodes_grad(ctl, table, spread, 0, 2, behind=sends)
    early_p, early_q = after(early_p, ctl), after(early_q, ctl)

    def piece(i):
        at, head, lanes = slice(i * rows, (i + 1) * rows), slice(TILE, TILE + 1), slice(i * EXTRA, (i + 1) * EXTRA)
        more_p, more_q = (early_p[:rows], early_q) if i == 3 else (late_p[at], late_q[at])
        p = total(kept[0, at, :half], got[0, at, :half], got_p[0, at], more_p)
        q = total(kept[0, at, half:], got[0, at, half:], got_q[0, at], more_q)
        ends = total(kept[0, head, lanes], got[0, head, lanes], got_p[0, head, lanes], early_p[rows : rows + 1, lanes])
        return jnp.concatenate([p, q, jnp.pad(ends, ((0, rows - 1), (0, 0)))], axis=1)

    third = piece(3).astype(BF16)
    far = swap(third, Z1)
    out, ctl = nodes_grad(ctl, table, spread, 2, 2, out, behind=(third,))
    far, late_p, late_q = after(far, ctl), after(late_p, ctl), after(late_q, ctl)
    second, first = (piece(2) + far.astype(F32)).astype(BF16), piece(1).astype(BF16)
    mid, near = swap(second, Z2), swap(first, Z1)
    out, ctl = nodes_grad(ctl, table, spread, 4, steps - 4, out, behind=(second, first))
    near, mid = after(near, ctl), after(mid, ctl)
    own_rows = piece(0)
    weight_grad = total(own_rows[:, :m], near[:, :m], mid[:, :m])
    ends = total(own_rows[0, m:], near[0, m:], mid[0, m:])
    return act, out, weight_grad, jnp.where(odd, ends[rows:], ends[:rows])


def general(nodes, weight, bias, neighbours, degree, counts, cotangent):
    ctl = cat(jnp.zeros_like(counts), counts)
    nb = neighbours.T
    deg = degree[None, :]
    steps = nodes.shape[0] // TILE
    full = lax.all_gather(weight, AXES, axis=0, tiled=True)
    bias_full = lax.all_gather(bias, AXES, axis=0, tiled=True).astype(F32)[None, :]
    table, _ = neighbour_table(ctl, nb, deg)
    agg, _, table = aggregate(ctl, deg, table, nodes, 0, steps)
    act, grad, bias_sum, _, agg = forward(ctl, agg, full, bias_full, cotangent)
    term = lax.dot_general(agg, grad, TN, preferred_element_type=F32)
    weight_grad = lax.psum_scatter(term, AXES, scatter_dimension=0, tiled=True)
    bias_grad = lax.psum_scatter(bias_sum[0], AXES, scatter_dimension=0, tiled=True)
    spread, _ = agg_grad(ctl, deg, grad, full)
    out, _ = nodes_grad(ctl, table, spread, 0, steps)
    return act, out, weight_grad, bias_grad


def solution(mesh):
    both = P(AXES, None)
    one = P(AXES)
    cube = (mesh.shape["clus"], mesh.shape["rep"]) == (8, 4)
    return jax.shard_map(
        fast if cube else general,
        mesh=mesh,
        in_specs=(both, both, one, both, one, one, both),
        out_specs=(both, both, both, one),
        check_vma=False,
    )
```
